256 devices in a mesh: row: 32 (over y, z), col: 8 (over x, core).
Axes of the slice: x: 4, y: 4, z: 8, core: 2. Of those that a mesh axis runs over, the one named last changes fastest.
Arguments:
- points: float32 [16, 32768], P(None, ('col', 'row')), may hold values from -6 to 6
- right_sides: float32 [17, 32768], P(None, ('col', 'row')), may hold values from -40 to 40
Outputs:
- solution_field: float32 [17, 32768], P(None, ('col', 'row'))
- residual: float32 [17, 32768], P(None, ('col', 'row'))
The draws below stay inside these ranges and needn't reach their ends.
All inputs are finite; a program needn't handle non-finite values.
Results may differ from the reference program's by a relative error of at most 0.0003.
Values sent between devices are 32-bit elements; how exact they have to be, the bound alone decides.
No kernel may reach another device: no remote copies, remote signals or barrier semaphores. Data moves between devices by JAX's collectives and lax.ppermute only.
A program may use at most 64 MiB of HBM per device.

```python
import jax
import jax.numpy as jnp
from jax import lax

FEATS = 16
NRHS = 17
ITERS = 2
NPTS = 32768


def draw_right_sides(key, part):
    key = jax.random.fold_in(key, 11)
    position = jnp.arange(NPTS).astype(jnp.float32)
    rising = 1.0 + 2.0 * position / NPTS
    values = jax.random.truncated_normal(key, -4.0, 4.0, (NRHS, NPTS)) * rising[None, :]
    return values.astype(jnp.float32)


def levels(key, dims, cuts, smallest, high):
    def one(axis_at, parts):
        draws = jax.random.uniform(jax.random.fold_in(jax.random.fold_in(key, 6), axis_at), (parts,), jnp.float32, smallest / len(cuts), high / len(cuts))
        return jnp.repeat(jnp.exp(draws), dims[axis_at] // parts).reshape((-1,) + (1,) * (len(dims) - axis_at - 1))

    gain = one(*cuts[0])
    for cut in cuts[1:]:
        gain = gain * one(*cut)
    return gain


def gaussian(stream_key, shape, width, limit, cuts=(), held_as=jnp.bfloat16):
    gain = levels(stream_key, shape, cuts, -0.22, 0.18) if cuts else 1.0
    entries = jax.random.normal(stream_key, shape, jnp.float32) * width * gain
    return jnp.minimum(jnp.maximum(entries, -limit), limit).astype(held_as)


def setup_inputs(seed: int = 0) -> dict:
    arg_keys = jax.random.split(jax.random.key(seed), 3)
    points = gaussian(arg_keys[0], (FEATS, NPTS), 1.0, 6.0, ((1, 256),), jnp.float32)
    right_sides = draw_right_sides(jax.random.fold_in(arg_keys[2], 71), 0)
    return {"points": points, "right_sides": right_sides}


NOISE = 0.1
SCALE = 0.125


def kernel_block(row_points, col_points):
    products = lax.dot_general(row_points, col_points, (((0,), (0,)), ((), ())), precision=lax.Precision.HIGHEST, preferred_element_type=jnp.float32)
    row_norms = jnp.sum(row_points * row_points, axis=0)
    col_norms = jnp.sum(col_points * col_points, axis=0)
    return jnp.exp(-SCALE * (row_norms[:, None] + col_norms[None, :] - 2.0 * products))


def apply_operator(points, vectors):
    whole_count = points.shape[1]
    block_rows = 512 if whole_count % 512 == 0 else whole_count
    starts = (jnp.arange(whole_count // block_rows) * block_rows).astype(jnp.int32)

    def one_block(first_row):
        row_points = lax.dynamic_slice_in_dim(points, first_row, block_rows, 1)
        kernel = kernel_block(row_points, points)
        return lax.dot_general(vectors, kernel, (((1,), (1,)), ((), ())), precision=lax.Precision.HIGHEST, preferred_element_type=jnp.float32)

    pieces = lax.map(one_block, starts)
    return jnp.transpose(pieces, (1, 0, 2)).reshape(vectors.shape) + NOISE * vectors


def reference(points, right_sides):
    solution_field = jnp.zeros_like(right_sides)
    residual = right_sides
    direction = right_sides
    norm_now = jnp.sum(residual * residual, axis=1)
    for iteration in range(ITERS):
        mapped = apply_operator(points, direction)
        step_size = norm_now / jnp.sum(direction * mapped, axis=1)
        solution_field = solution_field + step_size[:, None] * direction
        residual = residual - step_size[:, None] * mapped
        if iteration + 1 < ITERS:
            norm_next = jnp.sum(residual * residual, axis=1)
            direction = residual + (norm_next / norm_now)[:, None] * direction
            norm_now = norm_next
    return solution_field, residual
```

```python
import functools
import math

import jax
import jax.numpy as jnp
import numpy as np
from jax import lax
from jax.experimental import pallas as pl
from jax.experimental.pallas import tpu as pltpu
from jax.sharding import PartitionSpec as P

AXES = ("row", "col")
NOISE = 0.1
SCALE = 0.125
COEF = SCALE * math.log2(math.e)
F32 = jnp.float32
BF16 = jnp.bfloat16

DIMS = (("y", 4), ("w", 4), ("p", 2), ("x", 4), ("c", 2))
NAMES = [n for n, _ in DIMS]
IDS = np.arange(256).reshape([s for _, s in DIMS])


def send_by(**shift):
    target = IDS
    for name, amount in shift.items():
        target = np.roll(target, -amount, axis=NAMES.index(name))
    return list(zip(IDS.reshape(-1).tolist(), target.reshape(-1).tolist()))


def groups_over(*names):
    rest = [n for n in NAMES if n not in names]
    order = [NAMES.index(n) for n in rest + list(names)]
    size = int(np.prod([dict(DIMS)[n] for n in names]))
    return IDS.transpose(order).reshape(-1, size).tolist()


def split3(value):
    first = value.astype(BF16).astype(F32)
    rest = value - first
    second = rest.astype(BF16).astype(F32)
    return first, second, (rest - second).astype(BF16).astype(F32)


def norm_rows(points, norm_first):
    norm = -COEF * jnp.sum(points * points, axis=0, keepdims=True)
    parts = split3(norm)
    index = lax.broadcasted_iota(jnp.int32, points.shape, 0)
    base = 0 if norm_first else 3
    ones = 3 - base
    rows = jnp.where((index >= ones) & (index < ones + 3), 1.0, 0.0)
    for k in range(3):
        rows = jnp.where(index == base + k, parts[k], rows)
    return rows


def left_rows(points):
    a, b, c = split3(points * (2.0 * COEF))
    return jnp.concatenate(
        [a, a, b, b, a, c, norm_rows(points, True), jnp.zeros_like(a)], axis=0
    )


def right_rows(points):
    a, b, c = split3(points)
    return jnp.concatenate(
        [a, b, a, b, c, a, norm_rows(points, False), jnp.zeros_like(a)], axis=0
    )


def pad_rows(value, rows):
    return jnp.concatenate(
        [value, jnp.zeros((rows - value.shape[0], value.shape[1]), value.dtype)], axis=0
    )


def first_kernel(
    own_ref, by_c_ref, by_p_ref, x1_ref, x2_ref, x3_ref, col_ref,
    high_ref, low_ref, keep_ref, send_ref, left_ref, total_ref,
):
    step = pl.program_id(0)

    @pl.when(step == 0)
    def _():
        blocks = [
            jnp.concatenate([own_ref[...], by_c_ref[...], by_p_ref[...]], axis=1),
            x1_ref[...], x2_ref[...], x3_ref[...],
        ]
        for dx in range(4):
            rows = left_rows(blocks[dx]).T.astype(BF16)
            for dp in range(2):
                for dc in range(2):
                    low = (dp * 2 + dc) * 128
                    at = (dc * 8 + dp * 4 + dx) * 128
                    left_ref[at : at + 128, :] = rows[low : low + 128, :]
        total_ref[...] = jnp.zeros_like(total_ref)

    block = jnp.concatenate([col_ref[0], col_ref[1]], axis=1)
    right = right_rows(block[:16]).astype(BF16)
    parts = split3(block[16:])
    vectors = pad_rows(
        jnp.concatenate([pad_rows(part, 32) for part in parts], axis=0), 128
    ).T.astype(BF16)
    for chunk in range(8):
        at = pl.ds(chunk * 256, 256)
        kernel = jnp.exp2(jnp.dot(left_ref[at, :], right, preferred_element_type=F32))
        high = kernel.astype(BF16)
        low = (kernel - high.astype(F32)).astype(BF16)
        high_ref[at, :] = high
        low_ref[at, :] = low
        total_ref[at, :] += jnp.dot(
            high, vectors, preferred_element_type=F32
        ) + jnp.dot(low, vectors, preferred_element_type=F32)

    @pl.when(step == pl.num_programs(0) - 1)
    def _():
        for half, out_ref in enumerate((keep_ref, send_ref)):
            total = total_ref[half * 1024 : (half + 1) * 1024, :].T
            out_ref[...] = total[0:17] + total[32:49] + total[64:81]


def second_kernel(own_ref, by_p_ref, by_c_ref, high_ref, low_ref, out_ref, left_ref):
    @pl.when(pl.program_id(0) == 0)
    def _():
        vectors = jnp.concatenate([own_ref[...], by_p_ref[...], by_c_ref[...]], axis=1)
        left_ref[...] = jnp.concatenate(
            [pad_rows(part, 32) for part in split3(vectors)], axis=0
        ).astype(BF16)

    left = left_ref[...]
    total = jnp.dot(left, high_ref[...], preferred_element_type=F32) + jnp.dot(
        left, low_ref[...], preferred_element_type=F32
    )
    total = total[0:17] + total[32:49] + total[64:81]
    out_ref[0] = total[:, :128]
    out_ref[1] = total[:, 128:]


def dots_kernel(parts_ref, sides_ref, image_ref, out_first_ref, out_second_ref, dots_ref):
    sides = sides_ref[...]
    first = image_ref[:, :128] - sides
    second = jnp.sum(parts_ref[...], axis=0) - image_ref[:, :128] - first
    out_first_ref[...] = first
    out_second_ref[...] = second
    rows = jnp.concatenate(
        [pad_rows(t, 32) for t in (sides * sides, sides * first, first * first, first * second)],
        axis=0,
    )
    dots_ref[...] = jnp.sum(rows.T, axis=0, keepdims=True)


def last_kernel(dots_ref, sides_ref, first_ref, second_ref, solution_ref, residual_ref):
    dots = jnp.sum(dots_ref[...], axis=0)
    table = jnp.broadcast_to(dots, (128, 128)).T
    g0, g1, g2, g3 = (table[32 * k : 32 * k + 17] for k in range(4))
    diagonal = 1.0 + NOISE
    sides, first, second = sides_ref[...], first_ref[...], second_ref[...]
    step = g0 / (g1 + diagonal * g0)
    ratio = g1 / g0
    residual = step * (ratio * sides - first)
    norm = step * step * (g2 - ratio * g1)
    turn = norm / g0
    weight = step * ratio + turn
    direction = residual + turn * sides
    curve = (
        weight * weight * g1
        - 2.0 * weight * step * g2
        + step * step * g3
        + diagonal * (norm + turn * turn * g0)
    )
    step_next = norm / curve
    mapped = weight * first - step * second + diagonal * direction
    solution_ref[...] = step * sides + step_next * direction
    residual_ref[...] = residual - step_next * mapped


def whole(*shape):
    return pl.BlockSpec(shape, lambda i: (0,) * len(shape))


def per_device(points, right_sides):
    permute = functools.partial(lax.ppermute, axis_name=AXES)
    swap_c = send_by(c=1)
    swap_p = send_by(p=1)
    from_x = [send_by(x=-k) for k in (1, 2, 3)]
    col_groups = groups_over("y", "w")
    exchange = functools.partial(
        lax.all_to_all, axis_name=AXES, split_axis=0, concat_axis=0, tiled=True
    )

    by_c = permute(points, perm=swap_c)
    pair = jnp.concatenate([points, by_c], axis=1)
    by_p = permute(pair, perm=swap_p)
    four = jnp.concatenate([pair, by_p], axis=1)
    by_x = [permute(four, perm=p) for p in from_x]
    mine = jnp.concatenate([points, right_sides], axis=0)
    columns = exchange(
        jnp.broadcast_to(mine[None], (16, 33, 128)), axis_index_groups=col_groups
    )

    high, low, keep, send = pl.pallas_call(
        first_kernel,
        grid=(8,),
        in_specs=[
            whole(16, 128), whole(16, 128), whole(16, 256),
            whole(16, 512), whole(16, 512), whole(16, 512),
            pl.BlockSpec((2, 33, 128), lambda i: (i, 0, 0)),
        ],
        out_specs=[
            pl.BlockSpec((2048, 256), lambda i: (0, i)),
            pl.BlockSpec((2048, 256), lambda i: (0, i)),
            whole(17, 1024), whole(17, 1024),
        ],
        out_shape=[
            jax.ShapeDtypeStruct((2048, 2048), BF16),
            jax.ShapeDtypeStruct((2048, 2048), BF16),
            jax.ShapeDtypeStruct((17, 1024), F32),
            jax.ShapeDtypeStruct((17, 1024), F32),
        ],
        scratch_shapes=[pltpu.VMEM((2048, 128), BF16), pltpu.VMEM((2048, 128), F32)],
        compiler_params=pltpu.CompilerParams(vmem_limit_bytes=32 * 1024 * 1024),
        name="tile",
    )(points, by_c, by_p, *by_x, columns)

    half = keep + permute(send, perm=swap_c)
    quarter = half[:, :512] + permute(half[:, 512:], perm=swap_p)
    image = quarter
    for k, p in zip((1, 2, 3), from_x):
        image = image + jnp.roll(permute(quarter, perm=p), k * 128, axis=1)
    image_p = permute(image, perm=swap_p)
    image_c = permute(jnp.concatenate([image, image_p], axis=1), perm=swap_c)

    parts = pl.pallas_call(
        second_kernel,
        grid=(8,),
        in_specs=[
            whole(17, 512), whole(17, 512), whole(17, 1024),
            pl.BlockSpec((2048, 256), lambda i: (0, i)),
            pl.BlockSpec((2048, 256), lambda i: (0, i)),
        ],
        out_specs=pl.BlockSpec((2, 17, 128), lambda i: (i, 0, 0)),
        out_shape=jax.ShapeDtypeStruct((16, 17, 128), F32),
        scratch_shapes=[pltpu.VMEM((96, 2048), BF16)],
        compiler_params=pltpu.CompilerParams(vmem_limit_bytes=32 * 1024 * 1024),
        name="transposed",
    )(image, image_p, image_c, high, low)

    pieces = exchange(parts, axis_index_groups=col_groups)
    vector = jax.ShapeDtypeStruct((17, 128), F32)
    first, second, dots = pl.pallas_call(
        dots_kernel,
        out_shape=[vector, vector, jax.ShapeDtypeStruct((1, 128), F32)],
        name="dots",
    )(pieces, right_sides, image)
    all_dots = exchange(jnp.broadcast_to(dots[None], (256, 1, 128)))
    return pl.pallas_call(last_kernel, out_shape=[vector, vector], name="finish")(
        all_dots, right_sides, first, second
    )


def solution(mesh):
    spec = P(None, ("col", "row"))
    return jax.shard_map(
        lambda p, r: tuple(per_device(p, r)),
        mesh=mesh,
        in_specs=(spec, spec),
        out_specs=(spec, spec),
        check_vma=False,
    )
```

```python
import functools
import math

import jax
import jax.numpy as jnp
import numpy as np
from jax import lax
from jax.experimental import pallas as pl
from jax.experimental.pallas import tpu as pltpu
from jax.sharding import PartitionSpec as P

AXES = ("row", "col")
NOISE = 0.1
SCALE = 0.125
COEF = SCALE * math.log2(math.e)
F32 = jnp.float32
BF16 = jnp.bfloat16

DIMS = (("y", 4), ("u", 2), ("v", 2), ("p", 2), ("x", 4), ("c", 2))
NAMES = [n for n, _ in DIMS]
IDS = np.arange(256).reshape([s for _, s in DIMS])
FAR = (("v",), ("u",), ("u", "v"))


def swap(*names):
    target = np.flip(IDS, [NAMES.index(n) for n in names])
    return list(zip(IDS.reshape(-1).tolist(), target.reshape(-1).tolist()))


def groups_over(*names):
    rest = [n for n in NAMES if n not in names]
    order = [NAMES.index(n) for n in rest + list(names)]
    size = int(np.prod([dict(DIMS)[n] for n in names]))
    return IDS.transpose(order).reshape(-1, size).tolist()


def split3(value):
    first = value.astype(BF16).astype(F32)
    rest = value - first
    second = rest.astype(BF16).astype(F32)
    return first, second, (rest - second).astype(BF16).astype(F32)


def norm_rows(points, norm_first):
    norm = -COEF * jnp.sum(points * points, axis=0, keepdims=True)
    parts = split3(norm)
    index = lax.broadcasted_iota(jnp.int32, points.shape, 0)
    base = 0 if norm_first else 3
    ones = 3 - base
    rows = jnp.where((index >= ones) & (index < ones + 3), 1.0, 0.0)
    for k in range(3):
        rows = jnp.where(index == base + k, parts[k], rows)
    return rows


def left_rows(points):
    a, b, c = split3(points * (2.0 * COEF))
    return jnp.concatenate(
        [a, a, b, b, a, c, norm_rows(points, True), jnp.zeros_like(a)], axis=0
    )


def right_rows(points):
    a, b, c = split3(points)
    return jnp.concatenate(
        [a, b, a, b, c, a, norm_rows(points, False), jnp.zeros_like(a)], axis=0
    )


def pad_rows(value, rows):
    return jnp.concatenate(
        [value, jnp.zeros((rows - value.shape[0], value.shape[1]), value.dtype)], axis=0
    )


def tile_rows(left_ref, right_ref, vectors_ref, high_ref, low_ref, total_ref):
    count, width = high_ref.shape
    for column in range(0, width, 512):
        across = slice(column, column + 512)
        right, vectors = right_ref[:, across], vectors_ref[across, :]
        for row in range(0, count, 512):
            down = slice(row, row + 512)
            kernel = jnp.exp2(jnp.dot(left_ref[down, :], right, preferred_element_type=F32))
            high = kernel.astype(BF16)
            low = (kernel - high.astype(F32)).astype(BF16)
            high_ref[down, across] = high
            low_ref[down, across] = low
            part = jnp.dot(high, vectors, preferred_element_type=F32) + jnp.dot(
                low, vectors, preferred_element_type=F32
            )
            total_ref[down, :] = part if column == 0 else total_ref[down, :] + part


def sum_parts(total):
    return total[0:17] + total[32:49] + total[64:81]


def first_kernel(
    own_ref, by_c_ref, by_p_ref, v_ref, u_ref, uv_ref, columns_ref,
    high_ref, low_ref, out_ref, right_ref, vectors_ref, near_ref, next_ref,
    left_ref, total_ref,
):
    blocks = [
        jnp.concatenate([own_ref[...], by_c_ref[...], by_p_ref[...]], axis=1),
        v_ref[...], u_ref[...], uv_ref[...],
    ]
    for far in range(4):
        rows = left_rows(blocks[far]).T.astype(BF16)
        at = far * 128
        near_ref[at : at + 128, :] = rows[0:128, :]
        next_ref[at : at + 128, :] = rows[256:384, :]
        left_ref[at : at + 128, :] = rows[128:256, :]
        left_ref[512 + at : 640 + at, :] = rows[384:512, :]
    for group in range(4):
        block = jnp.concatenate([columns_ref[group * 4 + k] for k in range(4)], axis=1)
        at = slice(group * 512, group * 512 + 512)
        right_ref[:, at] = right_rows(block[:16]).astype(BF16)
        parts = [pad_rows(part, 32) for part in split3(block[16:])]
        vectors = pad_rows(jnp.concatenate(parts, axis=0), 128)
        vectors_ref[at, :] = vectors.T.astype(BF16)
    tile_rows(left_ref, right_ref, vectors_ref, high_ref, low_ref, total_ref)
    out_ref[...] = sum_parts(total_ref[...].T)


def more_kernel(left_ref, right_ref, vectors_ref, high_ref, low_ref, out_ref, total_ref):
    tile_rows(left_ref, right_ref, vectors_ref, high_ref, low_ref, total_ref)
    out_ref[...] = sum_parts(total_ref[...].T)


def transposed_kernel(image_ref, high_ref, low_ref, *rest_refs):
    out_ref = rest_refs[-1]
    left = jnp.concatenate(
        [pad_rows(part, 32) for part in split3(image_ref[...])], axis=0
    ).astype(BF16)
    total = jnp.dot(left, high_ref[...], preferred_element_type=F32) + jnp.dot(
        left, low_ref[...], preferred_element_type=F32
    )
    total = sum_parts(total)
    for k in range(16):
        piece = total[:, k * 128 : (k + 1) * 128]
        out_ref[k] = piece if len(rest_refs) == 1 else rest_refs[0][k] + piece


def dots_kernel(parts_ref, sides_ref, image_ref, out_first_ref, out_second_ref, dots_ref):
    sides = sides_ref[...]
    image = image_ref[:, :128]
    first = image - sides
    second = jnp.sum(parts_ref[...], axis=0) - image - first
    out_first_ref[...] = first
    out_second_ref[...] = second
    rows = jnp.concatenate(
        [pad_rows(t, 32) for t in (sides * sides, sides * first, first * first, first * second)],
        axis=0,
    )
    dots = jnp.sum(rows.T, axis=0, keepdims=True)
    dots_ref[...] = jnp.broadcast_to(dots[None], dots_ref.shape)


def last_kernel(dots_ref, sides_ref, first_ref, second_ref, solution_ref, residual_ref):
    dots = jnp.sum(dots_ref[...], axis=0)
    table = jnp.broadcast_to(dots, (128, 128)).T
    g0, g1, g2, g3 = (table[32 * k : 32 * k + 17] for k in range(4))
    diagonal = 1.0 + NOISE
    sides, first, second = sides_ref[...], first_ref[...], second_ref[...]
    step = g0 / (g1 + diagonal * g0)
    ratio = g1 / g0
    residual = step * (ratio * sides - first)
    norm = step * step * (g2 - ratio * g1)
    turn = norm / g0
    weight = step * ratio + turn
    direction = residual + turn * sides
    curve = (
        weight * weight * g1
        - 2.0 * weight * step * g2
        + step * step * g3
        + diagonal * (norm + turn * turn * g0)
    )
    step_next = norm / curve
    mapped = weight * first - step * second + diagonal * direction
    solution_ref[...] = step * sides + step_next * direction
    residual_ref[...] = residual - step_next * mapped


VMEM = pl.BlockSpec(memory_space=pltpu.VMEM)


def call(kernel, name, out_shape, scratch=(), flops=0, transcendentals=0):
    return pl.pallas_call(
        kernel,
        out_shape=out_shape,
        scratch_shapes=scratch,
        compiler_params=pltpu.CompilerParams(vmem_limit_bytes=28 * 1024 * 1024),
        cost_estimate=pl.CostEstimate(
            flops=flops, bytes_accessed=0, transcendentals=transcendentals
        ),
        name=name,
    )


def per_device(points, right_sides):
    permute = functools.partial(lax.ppermute, axis_name=AXES)
    exchange = functools.partial(
        lax.all_to_all, axis_name=AXES, split_axis=0, concat_axis=0, tiled=True
    )
    column_groups = groups_over("y", "x")
    swap_c, swap_p = swap("c"), swap("p")
    swap_far = [swap(*names) for names in FAR]

    by_c = permute(points, perm=swap_c)
    pair = jnp.concatenate([points, by_c], axis=1)
    by_p = permute(pair, perm=swap_p)
    four = jnp.concatenate([pair, by_p], axis=1)
    by_far = [permute(four, perm=p) for p in swap_far]
    mine = jnp.concatenate([points, right_sides], axis=0)
    columns = exchange(
        jnp.broadcast_to(mine[None], (16, 33, 128)), axis_index_groups=column_groups
    )

    def shape(rows, width, dtype=F32):
        return jax.ShapeDtypeStruct((rows, width), dtype)

    def tile(rows):
        return pltpu.VMEM((rows, 2048), BF16)

    high_c, low_c, send_c, right, vectors, near, following = call(
        first_kernel,
        "first",
        [
            tile(1024), tile(1024), shape(17, 1024), shape(128, 2048, BF16),
            shape(2048, 128, BF16), shape(512, 128, BF16), shape(512, 128, BF16),
        ],
        scratch=[pltpu.VMEM((1024, 128), BF16), pltpu.VMEM((1024, 128), F32)],
        flops=1024 * 2048 * 128 * 6,
        transcendentals=1024 * 2048,
    )(points, by_c, by_p, *by_far, columns)
    more = functools.partial(
        call, more_kernel,
        out_shape=[tile(512), tile(512), shape(17, 512)],
        scratch=[pltpu.VMEM((512, 128), F32)],
        flops=512 * 2048 * 128 * 6,
        transcendentals=512 * 2048,
    )
    from_c = permute(send_c, perm=swap_c)
    high_p, low_p, send_p = more(name="second")(following, right, vectors)
    from_p = permute(send_p + from_c[:, 512:], perm=swap_p)
    high, low, keep = more(name="third")(near, right, vectors)
    share = keep + from_c[:, :512] + from_p
    image = share
    for distance, p in enumerate(swap_far, 1):
        other = permute(share, perm=p)
        image = image + jnp.concatenate(
            [other[:, (k ^ distance) * 128 : (k ^ distance) * 128 + 128] for k in range(4)],
            axis=1,
        )

    def transposed(name, rows):
        return call(
            transposed_kernel, name, jax.ShapeDtypeStruct((16, 17, 128), F32),
            flops=rows * 2048 * 128 * 4,
        )

    image_p = permute(image, perm=swap_p)
    parts = transposed("near", 512)(image, high, low)
    image_c = permute(jnp.concatenate([image, image_p], axis=1), perm=swap_c)
    parts = transposed("next", 512)(image_p, high_p, low_p, parts)
    parts = transposed("other", 1024)(image_c, high_c, low_c, parts)
    pieces = exchange(parts, axis_index_groups=column_groups)

    vector = shape(17, 128)
    first, second, dots = call(
        dots_kernel, "dots", [vector, vector, jax.ShapeDtypeStruct((256, 1, 128), F32)]
    )(pieces, right_sides, image)
    all_dots = exchange(dots)
    return call(last_kernel, "finish", [vector, vector])(
        all_dots, right_sides, first, second
    )


def solution(mesh):
    spec = P(None, ("col", "row"))
    return jax.shard_map(
        lambda p, r: tuple(per_device(p, r)),
        mesh=mesh,
        in_specs=(spec, spec),
        out_specs=(spec, spec),
        check_vma=False,
    )
```

```python
import functools
import math

import jax
import jax.numpy as jnp
import numpy as np
from jax import lax
from jax.experimental import pallas as pl
from jax.experimental.pallas import tpu as pltpu
from jax.sharding import PartitionSpec as P

AXES = ("row", "col")
NOISE = 0.1
SCALE = 0.125
COEF = SCALE * math.log2(math.e)
F32 = jnp.float32
BF16 = jnp.bfloat16

DIMS = (("y", 4), ("u", 2), ("v", 2), ("p", 2), ("x", 4), ("c", 2))
NAMES = [n for n, _ in DIMS]
IDS = np.arange(256).reshape([s for _, s in DIMS])


def swap(*names):
    target = np.flip(IDS, [NAMES.index(n) for n in names])
    return list(zip(IDS.reshape(-1).tolist(), target.reshape(-1).tolist()))


def groups_over(*names):
    rest = [n for n in NAMES if n not in names]
    order = [NAMES.index(n) for n in rest + list(names)]
    size = int(np.prod([dict(DIMS)[n] for n in names]))
    return IDS.transpose(order).reshape(-1, size).tolist()


def split3(value):
    first = value.astype(BF16).astype(F32)
    rest = value - first
    second = rest.astype(BF16).astype(F32)
    return first, second, (rest - second).astype(BF16).astype(F32)


def norm_rows(points, norm_first):
    norm = -COEF * jnp.sum(points * points, axis=0, keepdims=True)
    parts = split3(norm)
    index = lax.broadcasted_iota(jnp.int32, points.shape, 0)
    base = 0 if norm_first else 3
    ones = 3 - base
    rows = jnp.where((index >= ones) & (index < ones + 3), 1.0, 0.0)
    for k in range(3):
        rows = jnp.where(index == base + k, parts[k], rows)
    return rows


def left_rows(points):
    a, b, c = split3(points * (2.0 * COEF))
    return jnp.concatenate(
        [a, a, b, b, a, c, norm_rows(points, True), jnp.zeros_like(a)], axis=0
    )


def right_rows(points):
    a, b, c = split3(points)
    return jnp.concatenate(
        [a, b, a, b, c, a, norm_rows(points, False), jnp.zeros_like(a)], axis=0
    )


def pad_rows(value, rows):
    return jnp.concatenate(
        [value, jnp.zeros((rows - value.shape[0], value.shape[1]), value.dtype)], axis=0
    )


def tile_rows(left_ref, right_ref, vectors_ref, high_ref, low_ref):
    contract = (((1,), (1,)), ((), ()))
    total = None
    for column in range(0, 2048, 1024):
        across = slice(column, column + 1024)
        kernel = jnp.exp2(
            jnp.dot(left_ref[...], right_ref[:, across], preferred_element_type=F32)
        )
        high = kernel.astype(BF16)
        low = (kernel - high.astype(F32)).astype(BF16)
        high_ref[:, across] = high
        low_ref[:, across] = low
        for part in (high, low):
            product = lax.dot_general(
                vectors_ref[:, across], part, contract, preferred_element_type=F32
            )
            total = product if total is None else total + product
    return sum_parts(total)


def sum_parts(total):
    return total[0:17] + total[32:49] + total[64:81]


def spread_kernel(points_hbm, sides_hbm, points_ref, sides_ref, copies_ref, done):
    copies = [
        pltpu.make_async_copy(points_hbm, points_ref, done.at[0]),
        pltpu.make_async_copy(sides_hbm, sides_ref, done.at[1]),
    ]
    for copy in copies:
        copy.start()
    for copy in copies:
        copy.wait()
    both = jnp.concatenate([points_ref[...], sides_ref[...]], axis=0)
    copies_ref[...] = jnp.broadcast_to(both[None], copies_ref.shape)


def make_left(points_ref, left_ref):
    left_ref[...] = left_rows(points_ref[...]).T.astype(BF16)


def make_right(columns_ref, right_ref, vectors_ref):
    for group in range(4):
        block = jnp.concatenate([columns_ref[group * 4 + k] for k in range(4)], axis=1)
        at = slice(group * 512, group * 512 + 512)
        right_ref[:, at] = right_rows(block[:16]).astype(BF16)
        parts = [pad_rows(part, 32) for part in split3(block[16:])]
        vectors_ref[:, at] = jnp.concatenate(parts, axis=0).astype(BF16)


def near_own_kernel(
    points_ref, columns_ref, high_ref, low_ref, out_ref, left_ref, right_ref, vectors_ref
):
    make_left(points_ref, left_ref)
    make_right(columns_ref, right_ref, vectors_ref)
    out_ref[...] = tile_rows(left_ref, right_ref, vectors_ref, high_ref, low_ref)


def next_own_kernel(
    points_ref, right_ref, vectors_ref, high_ref, low_ref, out_ref, left_ref
):
    make_left(points_ref, left_ref)
    out_ref[...] = tile_rows(left_ref, right_ref, vectors_ref, high_ref, low_ref)


def next_other_kernel(
    left_ref, columns_ref, before_ref, high_ref, low_ref, out_ref, right_ref, vectors_ref
):
    make_right(columns_ref, right_ref, vectors_ref)
    out_ref[...] = before_ref[...] + tile_rows(
        left_ref, right_ref, vectors_ref, high_ref, low_ref
    )


def near_other_kernel(
    left_ref, right_ref, vectors_ref, before_ref, high_ref, low_ref, out_ref
):
    out_ref[...] = before_ref[...] + tile_rows(
        left_ref, right_ref, vectors_ref, high_ref, low_ref
    )


def vector_parts(image_ref):
    return jnp.concatenate(
        [pad_rows(part, 32) for part in split3(image_ref[...])], axis=0
    ).astype(BF16)


def transposed_product(left, high_ref, low_ref):
    return sum_parts(
        jnp.dot(left, high_ref[...], preferred_element_type=F32)
        + jnp.dot(left, low_ref[...], preferred_element_type=F32)
    )


def near_transposed_kernel(
    image_ref, other_high_ref, other_low_ref, own_high_ref, own_low_ref, other_ref, own_ref
):
    left = vector_parts(image_ref)
    for high_ref, low_ref, out_ref in (
        (other_high_ref, other_low_ref, other_ref), (own_high_ref, own_low_ref, own_ref)
    ):
        total = transposed_product(left, high_ref, low_ref)
        for k in range(16):
            out_ref[k] = total[:, k * 128 : (k + 1) * 128]


def next_transposed_kernel(image_ref, high_ref, low_ref, before_ref, out_ref):
    total = transposed_product(vector_parts(image_ref), high_ref, low_ref)
    for k in range(16):
        out_ref[k] = before_ref[k] + total[:, k * 128 : (k + 1) * 128]


def dots_kernel(parts_ref, sides_ref, image_ref, out_first_ref, out_second_ref, dots_ref):
    sides = sides_ref[...]
    image = image_ref[:, :128]
    first = image - sides
    second = jnp.sum(parts_ref[...], axis=0) - image - first
    out_first_ref[...] = first
    out_second_ref[...] = second
    rows = jnp.concatenate(
        [pad_rows(t, 32) for t in (sides * sides, sides * first, first * first, first * second)],
        axis=0,
    )
    dots = jnp.sum(rows.T, axis=0, keepdims=True)
    dots_ref[...] = jnp.broadcast_to(dots[None], dots_ref.shape)


def last_kernel(dots_ref, sides_ref, first_ref, second_ref, solution_ref, residual_ref):
    dots = jnp.sum(dots_ref[...], axis=0)
    table = jnp.broadcast_to(dots, (128, 128)).T
    g0, g1, g2, g3 = (table[32 * k : 32 * k + 17] for k in range(4))
    diagonal = 1.0 + NOISE
    sides, first, second = sides_ref[...], first_ref[...], second_ref[...]
    step = g0 / (g1 + diagonal * g0)
    ratio = g1 / g0
    residual = step * (ratio * sides - first)
    norm = step * step * (g2 - ratio * g1)
    turn = norm / g0
    weight = step * ratio + turn
    direction = residual + turn * sides
    curve = (
        weight * weight * g1
        - 2.0 * weight * step * g2
        + step * step * g3
        + diagonal * (norm + turn * turn * g0)
    )
    step_next = norm / curve
    mapped = weight * first - step * second + diagonal * direction
    solution_ref[...] = step * sides + step_next * direction
    residual_ref[...] = residual - step_next * mapped


VMEM = pl.BlockSpec(memory_space=pltpu.VMEM)


def call(kernel, name, out_shape, scratch=(), flops=0, transcendentals=0):
    return pl.pallas_call(
        kernel,
        out_shape=out_shape,
        scratch_shapes=scratch,
        compiler_params=pltpu.CompilerParams(vmem_limit_bytes=28 * 1024 * 1024),
        cost_estimate=pl.CostEstimate(
            flops=flops, bytes_accessed=0, transcendentals=transcendentals
        ),
        name=name,
    )


def per_device(points, right_sides):
    permute = functools.partial(lax.ppermute, axis_name=AXES)
    exchange = functools.partial(
        lax.all_to_all, axis_name=AXES, split_axis=0, concat_axis=0, tiled=True
    )
    column_groups = groups_over("y", "x")
    swap_c, swap_p, swap_v, swap_uv = swap("c"), swap("p"), swap("v"), swap("u", "v")

    def shape(*dims, dtype=F32):
        return jax.ShapeDtypeStruct(dims, dtype)

    tiles = [pltpu.VMEM((512, 2048), BF16), pltpu.VMEM((512, 2048), BF16)]
    left_shape = shape(512, 128, dtype=BF16)
    right_shapes = [shape(128, 2048, dtype=BF16), shape(96, 2048, dtype=BF16)]
    make = functools.partial(
        call,
        flops=512 * 2048 * 128 * 6,
        transcendentals=512 * 2048,
    )

    by_v = permute(points, perm=swap_v)
    points, sides, copies = pl.pallas_call(
        spread_kernel,
        in_specs=[pl.BlockSpec(memory_space=pl.ANY)] * 2,
        out_shape=[
            pltpu.VMEM((16, 128), F32), pltpu.VMEM((17, 128), F32),
            pltpu.VMEM((16, 33, 128), F32),
        ],
        scratch_shapes=[pltpu.SemaphoreType.DMA((2,))],
        name="spread",
    )(points, right_sides)
    copies, by_v = lax.optimization_barrier((copies, by_v))
    pair = jnp.concatenate([points, by_v], axis=1)
    near_points = jnp.concatenate([pair, permute(pair, perm=swap_uv)], axis=1)
    own = exchange(copies, axis_index_groups=column_groups)

    next_points = permute(near_points, perm=swap_p)
    other = permute(own, perm=swap_c)
    *near_own, near_sum, near_left, right, vectors = make(
        near_own_kernel, "near_own",
        [*tiles, shape(17, 512), left_shape, *right_shapes],
    )(near_points, own)
    *next_own, next_sum, next_left = make(
        next_own_kernel, "next_own", [*tiles, shape(17, 512), left_shape]
    )(next_points, right, vectors)
    *next_other, next_sum, right, vectors = make(
        next_other_kernel, "next_other", [*tiles, shape(17, 512), *right_shapes]
    )(next_left, other, next_sum)
    from_p = permute(next_sum, perm=swap_p)
    *near_other, near_sum = make(
        near_other_kernel, "near_other", [*tiles, shape(17, 512)]
    )(near_left, right, vectors, near_sum)

    def turned(value, distance):
        return jnp.concatenate(
            [value[:, (k ^ distance) * 128 : (k ^ distance) * 128 + 128] for k in range(4)],
            axis=1,
        )

    total = near_sum + from_p
    total = total + turned(permute(total, perm=swap_v), 1)
    image = total + turned(permute(total, perm=swap_uv), 2)

    by_owner = shape(16, 17, 128)
    next_image = permute(image, perm=swap_p)
    other_part, own_part = call(
        near_transposed_kernel, "near_transposed", [by_owner, by_owner],
        flops=1024 * 2048 * 512,
    )(image, *near_other, *near_own)
    product = functools.partial(
        call, next_transposed_kernel, out_shape=by_owner, flops=512 * 2048 * 512
    )
    other_part = product(name="other_transposed")(next_image, *next_other, other_part)
    from_c = permute(other_part, perm=swap_c)
    own_part = product(name="own_transposed")(next_image, *next_own, own_part)
    pieces = exchange(own_part + from_c, axis_index_groups=column_groups)

    vector = shape(17, 128)
    first, second, dots = call(dots_kernel, "dots", [vector, vector, shape(256, 1, 128)])(
        pieces, sides, image
    )
    all_dots = exchange(dots)
    return call(last_kernel, "finish", [vector, vector])(
        all_dots, sides, first, second
    )


def solution(mesh):
    spec = P(None, ("col", "row"))
    return jax.shard_map(
        lambda p, r: tuple(per_device(p, r)),
        mesh=mesh,
        in_specs=(spec, spec),
        out_specs=(spec, spec),
        check_vma=False,
    )
```

```python
import functools
import math

import jax
import jax.numpy as jnp
import numpy as np
from jax import lax
from jax.experimental import pallas as pl
from jax.experimental.pallas import tpu as pltpu
from jax.sharding import PartitionSpec as P

AXES = ("row", "col")
NOISE = 0.1
SCALE = 0.125
COEF = SCALE * math.log2(math.e)
F32 = jnp.float32
BF16 = jnp.bfloat16

DIMS = (("y", 4), ("u", 2), ("v", 2), ("p", 2), ("x", 4), ("c", 2))
NAMES = [n for n, _ in DIMS]
IDS = np.arange(256).reshape([s for _, s in DIMS])


def swap(*names):
    target = np.flip(IDS, [NAMES.index(n) for n in names])
    return list(zip(IDS.reshape(-1).tolist(), target.reshape(-1).tolist()))


def groups_over(*names):
    rest = [n for n in NAMES if n not in names]
    order = [NAMES.index(n) for n in rest + list(names)]
    size = int(np.prod([dict(DIMS)[n] for n in names]))
    return IDS.transpose(order).reshape(-1, size).tolist()


def split3(value):
    first = value.astype(BF16).astype(F32)
    rest = value - first
    second = rest.astype(BF16).astype(F32)
    return first, second, (rest - second).astype(BF16).astype(F32)


def norm_rows(points, norm_first):
    norm = -COEF * jnp.sum(points * points, axis=0, keepdims=True)
    parts = split3(norm)
    index = lax.broadcasted_iota(jnp.int32, points.shape, 0)
    base = 0 if norm_first else 3
    ones = 3 - base
    rows = jnp.where((index >= ones) & (index < ones + 3), 1.0, 0.0)
    for k in range(3):
        rows = jnp.where(index == base + k, parts[k], rows)
    return rows


def left_rows(points):
    a, b, c = split3(points * (2.0 * COEF))
    return jnp.concatenate(
        [a, a, b, b, a, c, norm_rows(points, True), jnp.zeros_like(a)], axis=0
    )


def right_rows(points):
    a, b, c = split3(points)
    return jnp.concatenate(
        [a, b, a, b, c, a, norm_rows(points, False), jnp.zeros_like(a)], axis=0
    )


def pad_rows(value, rows):
    return jnp.concatenate(
        [value, jnp.zeros((rows - value.shape[0], value.shape[1]), value.dtype)], axis=0
    )


def tile_rows(left_ref, right_ref, vectors_ref, high_ref, low_ref):
    width = 256
    total, waiting = 0.0, None
    for column in range(0, 2048 + width, width):
        made = None
        if column < 2048:
            across = slice(column, column + width)
            kernel = jnp.exp2(
                jnp.dot(left_ref[...], right_ref[:, across], preferred_element_type=F32)
            )
            high = kernel.astype(BF16)
            low = (kernel - high.astype(F32)).astype(BF16)
            high_ref[:, across] = high
            low_ref[:, across] = low
            made = across, high, low
        if waiting:
            across, *parts = waiting
            for part in parts:
                total = total + lax.dot_general(
                    vectors_ref[:, across], part, (((1,), (1,)), ((), ())),
                    preferred_element_type=F32,
                )
        waiting = made
    return sum_parts(total)


def sum_parts(total):
    return total[0:17] + total[32:49] + total[64:81]


def spread_kernel(points_hbm, sides_hbm, points_ref, sides_ref, copies_ref, done):
    copies = [
        pltpu.make_async_copy(points_hbm, points_ref, done.at[0]),
        pltpu.make_async_copy(sides_hbm, sides_ref, done.at[1]),
    ]
    for copy in copies:
        copy.start()
    for copy in copies:
        copy.wait()
    both = jnp.concatenate([points_ref[...], sides_ref[...]], axis=0)
    copies_ref[...] = jnp.broadcast_to(both[None], copies_ref.shape)


def make_left(points_ref, left_ref):
    left_ref[...] = left_rows(points_ref[...]).T.astype(BF16)


def make_right(columns_ref, right_ref, vectors_ref):
    for group in range(4):
        block = jnp.concatenate([columns_ref[group * 4 + k] for k in range(4)], axis=1)
        at = slice(group * 512, group * 512 + 512)
        right_ref[:, at] = right_rows(block[:16]).astype(BF16)
        parts = [pad_rows(part, 32) for part in split3(block[16:])]
        vectors_ref[:, at] = jnp.concatenate(parts, axis=0).astype(BF16)


def near_own_kernel(
    points_ref, columns_ref, high_ref, low_ref, out_ref, left_ref, right_ref, vectors_ref
):
    make_left(points_ref, left_ref)
    make_right(columns_ref, right_ref, vectors_ref)
    out_ref[...] = tile_rows(left_ref, right_ref, vectors_ref, high_ref, low_ref)


def next_own_kernel(
    points_ref, right_ref, vectors_ref, high_ref, low_ref, out_ref, left_ref
):
    make_left(points_ref, left_ref)
    out_ref[...] = tile_rows(left_ref, right_ref, vectors_ref, high_ref, low_ref)


def next_other_kernel(
    left_ref, columns_ref, before_ref, high_ref, low_ref, out_ref, right_ref, vectors_ref
):
    make_right(columns_ref, right_ref, vectors_ref)
    out_ref[...] = before_ref[...] + tile_rows(
        left_ref, right_ref, vectors_ref, high_ref, low_ref
    )


def near_other_kernel(
    left_ref, right_ref, vectors_ref, before_ref, high_ref, low_ref, out_ref
):
    out_ref[...] = before_ref[...] + tile_rows(
        left_ref, right_ref, vectors_ref, high_ref, low_ref
    )


def vector_parts(image_ref):
    return jnp.concatenate(
        [pad_rows(part, 32) for part in split3(image_ref[...])], axis=0
    ).astype(BF16)


def transposed_product(left, high_ref, low_ref):
    return sum_parts(
        jnp.dot(left, high_ref[...], preferred_element_type=F32)
        + jnp.dot(left, low_ref[...], preferred_element_type=F32)
    )


def near_transposed_kernel(
    image_ref, other_high_ref, other_low_ref, own_high_ref, own_low_ref, other_ref, own_ref
):
    left = vector_parts(image_ref)
    for high_ref, low_ref, out_ref in (
        (other_high_ref, other_low_ref, other_ref), (own_high_ref, own_low_ref, own_ref)
    ):
        total = transposed_product(left, high_ref, low_ref)
        for k in range(16):
            out_ref[k] = total[:, k * 128 : (k + 1) * 128]


def next_transposed_kernel(image_ref, high_ref, low_ref, before_ref, out_ref):
    total = transposed_product(vector_parts(image_ref), high_ref, low_ref)
    for k in range(16):
        out_ref[k] = before_ref[k] + total[:, k * 128 : (k + 1) * 128]


def dots_kernel(parts_ref, sides_ref, image_ref, out_first_ref, out_second_ref, dots_ref):
    sides = sides_ref[...]
    image = image_ref[:, :128]
    first = image - sides
    second = jnp.sum(parts_ref[...], axis=0) - image - first
    out_first_ref[...] = first
    out_second_ref[...] = second
    rows = jnp.concatenate(
        [pad_rows(t, 32) for t in (sides * sides, sides * first, first * first, first * second)],
        axis=0,
    )
    dots_ref[...] = jnp.sum(rows.T, axis=0, keepdims=True)


def last_kernel(dots_ref, sides_ref, first_ref, second_ref, solution_ref, residual_ref):
    dots = jnp.sum(dots_ref[...], axis=0)
    table = jnp.broadcast_to(dots, (128, 128)).T
    g0, g1, g2, g3 = (table[32 * k : 32 * k + 17] for k in range(4))
    diagonal = 1.0 + NOISE
    sides, first, second = sides_ref[...], first_ref[...], second_ref[...]
    step = g0 / (g1 + diagonal * g0)
    ratio = g1 / g0
    residual = step * (ratio * sides - first)
    norm = step * step * (g2 - ratio * g1)
    turn = norm / g0
    weight = step * ratio + turn
    direction = residual + turn * sides
    curve = (
        weight * weight * g1
        - 2.0 * weight * step * g2
        + step * step * g3
        + diagonal * (norm + turn * turn * g0)
    )
    step_next = norm / curve
    mapped = weight * first - step * second + diagonal * direction
    solution_ref[...] = step * sides + step_next * direction
    residual_ref[...] = residual - step_next * mapped


VMEM = pl.BlockSpec(memory_space=pltpu.VMEM)


def call(kernel, name, out_shape, scratch=(), flops=0, transcendentals=0):
    return pl.pallas_call(
        kernel,
        out_shape=out_shape,
        scratch_shapes=scratch,
        compiler_params=pltpu.CompilerParams(vmem_limit_bytes=28 * 1024 * 1024),
        cost_estimate=pl.CostEstimate(
            flops=flops, bytes_accessed=0, transcendentals=transcendentals
        ),
        name=name,
    )


def per_device(points, right_sides):
    permute = functools.partial(lax.ppermute, axis_name=AXES)
    exchange = functools.partial(
        lax.all_to_all, axis_name=AXES, split_axis=0, concat_axis=0, tiled=True
    )
    column_groups = groups_over("y", "x")
    swap_c, swap_p, swap_v, swap_uv = swap("c"), swap("p"), swap("v"), swap("u", "v")

    def shape(*dims, dtype=F32):
        return jax.ShapeDtypeStruct(dims, dtype)

    tiles = [pltpu.VMEM((512, 2048), BF16), pltpu.VMEM((512, 2048), BF16)]
    left_shape = shape(512, 128, dtype=BF16)
    right_shapes = [shape(128, 2048, dtype=BF16), shape(96, 2048, dtype=BF16)]
    make = functools.partial(
        call,
        flops=512 * 2048 * 128 * 6,
        transcendentals=512 * 2048,
    )

    by_v = permute(points, perm=swap_v)
    points, sides, copies = pl.pallas_call(
        spread_kernel,
        in_specs=[pl.BlockSpec(memory_space=pl.ANY)] * 2,
        out_shape=[
            pltpu.VMEM((16, 128), F32), pltpu.VMEM((17, 128), F32),
            pltpu.VMEM((16, 33, 128), F32),
        ],
        scratch_shapes=[pltpu.SemaphoreType.DMA((2,))],
        name="spread",
    )(points, right_sides)
    pair = jnp.concatenate([points, by_v], axis=1)
    near_points = jnp.concatenate([pair, permute(pair, perm=swap_uv)], axis=1)
    own = exchange(copies, axis_index_groups=column_groups)
    next_points = permute(near_points, perm=swap_p)
    own, near_points = lax.optimization_barrier((own, near_points))

    other = permute(own, perm=swap_c)
    *near_own, near_sum, near_left, right, vectors = make(
        near_own_kernel, "near_own",
        [*tiles, shape(17, 512), left_shape, *right_shapes],
    )(near_points, own)
    *next_own, next_sum, next_left = make(
        next_own_kernel, "next_own", [*tiles, shape(17, 512), left_shape]
    )(next_points, right, vectors)
    *next_other, next_sum, right, vectors = make(
        next_other_kernel, "next_other", [*tiles, shape(17, 512), *right_shapes]
    )(next_left, other, next_sum)
    from_p = permute(next_sum, perm=swap_p)
    *near_other, near_sum = make(
        near_other_kernel, "near_other", [*tiles, shape(17, 512)]
    )(near_left, right, vectors, near_sum)

    def turned(value, distance):
        return jnp.concatenate(
            [value[:, (k ^ distance) * 128 : (k ^ distance) * 128 + 128] for k in range(4)],
            axis=1,
        )

    total = near_sum + from_p
    total = total + turned(permute(total, perm=swap_v), 1)
    image = total + turned(permute(total, perm=swap_uv), 2)

    by_owner = shape(16, 17, 128)
    next_image = permute(image, perm=swap_p)
    other_part, own_part = call(
        near_transposed_kernel, "near_transposed", [by_owner, by_owner],
        flops=1024 * 2048 * 512,
    )(image, *near_other, *near_own)
    product = functools.partial(
        call, next_transposed_kernel, out_shape=by_owner, flops=512 * 2048 * 512
    )
    other_part = product(name="other_transposed")(next_image, *next_other, other_part)
    from_c = permute(other_part, perm=swap_c)
    own_part = product(name="own_transposed")(next_image, *next_own, own_part)
    pieces = exchange(own_part + from_c, axis_index_groups=column_groups)

    vector = shape(17, 128)
    first, second, dots = call(dots_kernel, "dots", [vector, vector, shape(1, 128)])(
        pieces, sides, image
    )
    dots = dots + permute(dots, perm=swap_c)
    all_dots = exchange(
        jnp.broadcast_to(dots[None], (128, 1, 128)),
        axis_index_groups=groups_over("y", "u", "v", "p", "x"),
    )
    return call(last_kernel, "finish", [vector, vector])(
        all_dots, sides, first, second
    )


def solution(mesh):
    spec = P(None, ("col", "row"))
    return jax.shard_map(
        lambda p, r: tuple(per_device(p, r)),
        mesh=mesh,
        in_specs=(spec, spec),
        out_specs=(spec, spec),
        check_vma=False,
    )
```

```python
import functools
import math

import jax
import jax.numpy as jnp
import numpy as np
from jax import lax
from jax.experimental import pallas as pl
from jax.experimental.pallas import tpu as pltpu
from jax.sharding import PartitionSpec as P

AXES = ("row", "col")
NOISE = 0.1
SCALE = 0.125
COEF = SCALE * math.log2(math.e)
F32 = jnp.float32
BF16 = jnp.bfloat16

DIMS = (("y", 4), ("u", 2), ("v", 2), ("p", 2), ("x", 4), ("c", 2))
NAMES = [n for n, _ in DIMS]
IDS = np.arange(256).reshape([s for _, s in DIMS])


def swap(*names):
    target = np.flip(IDS, [NAMES.index(n) for n in names])
    return list(zip(IDS.reshape(-1).tolist(), target.reshape(-1).tolist()))


def groups_over(*names):
    rest = [n for n in NAMES if n not in names]
    order = [NAMES.index(n) for n in rest + list(names)]
    size = int(np.prod([dict(DIMS)[n] for n in names]))
    return IDS.transpose(order).reshape(-1, size).tolist()


def split3(value):
    first = value.astype(BF16).astype(F32)
    rest = value - first
    second = rest.astype(BF16).astype(F32)
    return first, second, (rest - second).astype(BF16).astype(F32)


def norm_rows(points, norm_first):
    norm = -COEF * jnp.sum(points * points, axis=0, keepdims=True)
    parts = split3(norm)
    index = lax.broadcasted_iota(jnp.int32, points.shape, 0)
    base = 0 if norm_first else 3
    ones = 3 - base
    rows = jnp.where((index >= ones) & (index < ones + 3), 1.0, 0.0)
    for k in range(3):
        rows = jnp.where(index == base + k, parts[k], rows)
    return rows


def left_rows(points):
    a, b, c = split3(points * (2.0 * COEF))
    return jnp.concatenate(
        [a, a, b, b, a, c, norm_rows(points, True), jnp.zeros_like(a)], axis=0
    )


def right_rows(points):
    a, b, c = split3(points)
    return jnp.concatenate(
        [a, b, a, b, c, a, norm_rows(points, False), jnp.zeros_like(a)], axis=0
    )


def pad_rows(value, rows):
    return jnp.concatenate(
        [value, jnp.zeros((rows - value.shape[0], value.shape[1]), value.dtype)], axis=0
    )


def tile_rows(left_ref, right_ref, vectors_ref, high_ref, low_ref):
    width = 256
    total, waiting = 0.0, None
    for column in range(0, 2048 + width, width):
        made = None
        if column < 2048:
            across = slice(column, column + width)
            kernel = jnp.exp2(
                jnp.dot(left_ref[...], right_ref[:, across], preferred_element_type=F32)
            )
            high = kernel.astype(BF16)
            low = (kernel - high.astype(F32)).astype(BF16)
            high_ref[:, across] = high
            low_ref[:, across] = low
            made = across, high, low
        if waiting:
            across, *parts = waiting
            for part in parts:
                total = total + lax.dot_general(
                    vectors_ref[:, across], part, (((1,), (1,)), ((), ())),
                    preferred_element_type=F32,
                )
        waiting = made
    return sum_parts(total)


def sum_parts(total):
    return total[0:17] + total[32:49] + total[64:81]


def spread_kernel(points_hbm, sides_hbm, points_ref, sides_ref, copies_ref, done):
    copies = [
        pltpu.make_async_copy(points_hbm, points_ref, done.at[0]),
        pltpu.make_async_copy(sides_hbm, sides_ref, done.at[1]),
    ]
    for copy in copies:
        copy.start()
    for copy in copies:
        copy.wait()
    for k in range(16):
        copies_ref[k, 0:16, :] = points_ref[...]
        copies_ref[k, 16:33, :] = sides_ref[...]


def make_left(points_ref, left_ref):
    left_ref[...] = left_rows(points_ref[...]).T.astype(BF16)


def make_right(columns_ref, right_ref, vectors_ref):
    for group in range(4):
        block = jnp.concatenate([columns_ref[group * 4 + k] for k in range(4)], axis=1)
        at = slice(group * 512, group * 512 + 512)
        right_ref[:, at] = right_rows(block[:16]).astype(BF16)
        parts = [pad_rows(part, 32) for part in split3(block[16:])]
        vectors_ref[:, at] = jnp.concatenate(parts, axis=0).astype(BF16)


def near_own_kernel(
    points_ref, columns_ref, high_ref, low_ref, out_ref, left_ref, right_ref, vectors_ref
):
    make_left(points_ref, left_ref)
    make_right(columns_ref, right_ref, vectors_ref)
    out_ref[...] = tile_rows(left_ref, right_ref, vectors_ref, high_ref, low_ref)


def next_own_kernel(
    points_ref, right_ref, vectors_ref, high_ref, low_ref, out_ref, left_ref
):
    make_left(points_ref, left_ref)
    out_ref[...] = tile_rows(left_ref, right_ref, vectors_ref, high_ref, low_ref)


def next_other_kernel(
    left_ref, columns_ref, before_ref, high_ref, low_ref, out_ref, right_ref, vectors_ref
):
    make_right(columns_ref, right_ref, vectors_ref)
    out_ref[...] = before_ref[...] + tile_rows(
        left_ref, right_ref, vectors_ref, high_ref, low_ref
    )


def near_other_kernel(
    left_ref, right_ref, vectors_ref, before_ref, high_ref, low_ref, out_ref
):
    out_ref[...] = before_ref[...] + tile_rows(
        left_ref, right_ref, vectors_ref, high_ref, low_ref
    )


def vector_parts(image_ref):
    return jnp.concatenate(
        [pad_rows(part, 32) for part in split3(image_ref[...])], axis=0
    ).astype(BF16)


def transposed_product(left, high_ref, low_ref):
    return sum_parts(
        jnp.dot(left, high_ref[...], preferred_element_type=F32)
        + jnp.dot(left, low_ref[...], preferred_element_type=F32)
    )


def near_transposed_kernel(
    image_ref, other_high_ref, other_low_ref, own_high_ref, own_low_ref, other_ref, own_ref
):
    left = vector_parts(image_ref)
    for high_ref, low_ref, out_ref in (
        (other_high_ref, other_low_ref, other_ref), (own_high_ref, own_low_ref, own_ref)
    ):
        total = transposed_product(left, high_ref, low_ref)
        for k in range(16):
            out_ref[k] = total[:, k * 128 : (k + 1) * 128]


def next_transposed_kernel(image_ref, high_ref, low_ref, before_ref, out_ref):
    total = transposed_product(vector_parts(image_ref), high_ref, low_ref)
    for k in range(16):
        out_ref[k] = before_ref[k] + total[:, k * 128 : (k + 1) * 128]


def dots_kernel(parts_ref, sides_ref, image_ref, out_first_ref, out_second_ref, dots_ref):
    sides = sides_ref[...]
    image = image_ref[:, :128]
    first = image - sides
    second = jnp.sum(parts_ref[...], axis=0) - image - first
    out_first_ref[...] = first
    out_second_ref[...] = second
    rows = jnp.concatenate(
        [pad_rows(t, 32) for t in (sides * sides, sides * first, first * first, first * second)],
        axis=0,
    )
    dots_ref[...] = jnp.sum(rows.T, axis=0, keepdims=True)


def last_kernel(dots_ref, sides_ref, first_ref, second_ref, solution_ref, residual_ref):
    dots = jnp.sum(dots_ref[...], axis=0)
    table = jnp.broadcast_to(dots, (128, 128)).T
    g0, g1, g2, g3 = (table[32 * k : 32 * k + 17] for k in range(4))
    diagonal = 1.0 + NOISE
    sides, first, second = sides_ref[...], first_ref[...], second_ref[...]
    step = g0 / (g1 + diagonal * g0)
    ratio = g1 / g0
    residual = step * (ratio * sides - first)
    norm = step * step * (g2 - ratio * g1)
    turn = norm / g0
    weight = step * ratio + turn
    direction = residual + turn * sides
    curve = (
        weight * weight * g1
        - 2.0 * weight * step * g2
        + step * step * g3
        + diagonal * (norm + turn * turn * g0)
    )
    step_next = norm / curve
    mapped = weight * first - step * second + diagonal * direction
    solution_ref[...] = step * sides + step_next * direction
    residual_ref[...] = residual - step_next * mapped


VMEM = pl.BlockSpec(memory_space=pltpu.VMEM)


def call(kernel, name, out_shape, scratch=(), flops=0, transcendentals=0):
    return pl.pallas_call(
        kernel,
        out_shape=out_shape,
        scratch_shapes=scratch,
        compiler_params=pltpu.CompilerParams(vmem_limit_bytes=28 * 1024 * 1024),
        cost_estimate=pl.CostEstimate(
            flops=flops, bytes_accessed=0, transcendentals=transcendentals
        ),
        name=name,
    )


def per_device(points, right_sides):
    permute = functools.partial(lax.ppermute, axis_name=AXES)
    exchange = functools.partial(
        lax.all_to_all, axis_name=AXES, split_axis=0, concat_axis=0, tiled=True
    )
    column_groups = groups_over("y", "x")
    swap_c, swap_p, swap_v, swap_uv = swap("c"), swap("p"), swap("v"), swap("u", "v")

    def shape(*dims, dtype=F32):
        return jax.ShapeDtypeStruct(dims, dtype)

    tiles = [pltpu.VMEM((512, 2048), BF16), pltpu.VMEM((512, 2048), BF16)]
    left_shape = shape(512, 128, dtype=BF16)
    right_shapes = [shape(128, 2048, dtype=BF16), shape(96, 2048, dtype=BF16)]
    make = functools.partial(
        call,
        flops=512 * 2048 * 128 * 6,
        transcendentals=512 * 2048,
    )

    by_v = permute(points, perm=swap_v)
    points, sides, copies = pl.pallas_call(
        spread_kernel,
        in_specs=[pl.BlockSpec(memory_space=pl.ANY)] * 2,
        out_shape=[
            pltpu.VMEM((16, 128), F32), pltpu.VMEM((17, 128), F32),
            pltpu.VMEM((16, 33, 128), F32),
        ],
        scratch_shapes=[pltpu.SemaphoreType.DMA((2,))],
        name="spread",
    )(points, right_sides)
    pair = jnp.concatenate([points, by_v], axis=1)
    near_points = jnp.concatenate([pair, permute(pair, perm=swap_uv)], axis=1)
    own = exchange(copies, axis_index_groups=column_groups)
    next_points = permute(near_points, perm=swap_p)
    own, near_points = lax.optimization_barrier((own, near_points))

    other = permute(own, perm=swap_c)
    *near_own, near_sum, near_left, right, vectors = make(
        near_own_kernel, "near_own",
        [*tiles, shape(17, 512), left_shape, *right_shapes],
    )(near_points, own)
    *next_own, next_sum, next_left = make(
        next_own_kernel, "next_own", [*tiles, shape(17, 512), left_shape]
    )(next_points, right, vectors)
    *next_other, next_sum, right, vectors = make(
        next_other_kernel, "next_other", [*tiles, shape(17, 512), *right_shapes]
    )(next_left, other, next_sum)
    from_p = permute(next_sum, perm=swap_p)
    *near_other, near_sum = make(
        near_other_kernel, "near_other", [*tiles, shape(17, 512)]
    )(near_left, right, vectors, near_sum)

    def turned(value, distance):
        return jnp.concatenate(
            [value[:, (k ^ distance) * 128 : (k ^ distance) * 128 + 128] for k in range(4)],
            axis=1,
        )

    total = near_sum + from_p
    image = total
    for distance, pairs in ((3, swap("u")), (2, swap_uv), (1, swap_v)):
        image = image + turned(permute(total, perm=pairs), distance)

    by_owner = shape(16, 17, 128)
    next_image = permute(image, perm=swap_p)
    other_part, own_part = call(
        near_transposed_kernel, "near_transposed", [by_owner, by_owner],
        flops=1024 * 2048 * 512,
    )(image, *near_other, *near_own)
    product = functools.partial(
        call, next_transposed_kernel, out_shape=by_owner, flops=512 * 2048 * 512
    )
    other_part = product(name="other_transposed")(next_image, *next_other, other_part)
    from_c = permute(other_part, perm=swap_c)
    own_part = product(name="own_transposed")(next_image, *next_own, own_part)
    pieces = exchange(own_part + from_c, axis_index_groups=column_groups)

    vector = shape(17, 128)
    first, second, dots = call(dots_kernel, "dots", [vector, vector, shape(1, 128)])(
        pieces, sides, image
    )
    dots = dots + permute(dots, perm=swap_c)
    all_dots = exchange(
        jnp.broadcast_to(dots[None], (128, 1, 128)),
        axis_index_groups=groups_over("y", "u", "v", "p", "x"),
    )
    return call(last_kernel, "finish", [vector, vector])(
        all_dots, sides, first, second
    )


def solution(mesh):
    spec = P(None, ("col", "row"))
    return jax.shard_map(
        lambda p, r: tuple(per_device(p, r)),
        mesh=mesh,
        in_specs=(spec, spec),
        out_specs=(spec, spec),
        check_vma=False,
    )
```

```python
import functools
import math

import jax
import jax.numpy as jnp
import numpy as np
from jax import lax
from jax.experimental import pallas as pl
from jax.experimental.pallas import tpu as pltpu
from jax.sharding import PartitionSpec as P

AXES = ("row", "col")
NOISE = 0.1
SCALE = 0.125
COEF = SCALE * math.log2(math.e)
F32 = jnp.float32
BF16 = jnp.bfloat16

DIMS = (("y", 4), ("u", 2), ("v", 2), ("p", 2), ("x", 4), ("c", 2))
NAMES = [n for n, _ in DIMS]
IDS = np.arange(256).reshape([s for _, s in DIMS])


def swap(*names):
    target = np.flip(IDS, [NAMES.index(n) for n in names])
    return list(zip(IDS.reshape(-1).tolist(), target.reshape(-1).tolist()))


def groups_over(*names):
    rest = [n for n in NAMES if n not in names]
    order = [NAMES.index(n) for n in rest + list(names)]
    size = int(np.prod([dict(DIMS)[n] for n in names]))
    return IDS.transpose(order).reshape(-1, size).tolist()


def split3(value):
    first = value.astype(BF16).astype(F32)
    rest = value - first
    second = rest.astype(BF16).astype(F32)
    return first, second, (rest - second).astype(BF16).astype(F32)


def norm_rows(points, norm_first):
    norm = -COEF * jnp.sum(points * points, axis=0, keepdims=True)
    parts = split3(norm)
    index = lax.broadcasted_iota(jnp.int32, points.shape, 0)
    base = 0 if norm_first else 3
    ones = 3 - base
    rows = jnp.where((index >= ones) & (index < ones + 3), 1.0, 0.0)
    for k in range(3):
        rows = jnp.where(index == base + k, parts[k], rows)
    return rows


def left_rows(points):
    a, b, c = split3(points * (2.0 * COEF))
    return jnp.concatenate(
        [a, a, b, b, a, c, norm_rows(points, True), jnp.zeros_like(a)], axis=0
    )


def right_rows(points):
    a, b, c = split3(points)
    return jnp.concatenate(
        [a, b, a, b, c, a, norm_rows(points, False), jnp.zeros_like(a)], axis=0
    )


def pad_rows(value, rows):
    return jnp.concatenate(
        [value, jnp.zeros((rows - value.shape[0], value.shape[1]), value.dtype)], axis=0
    )


def tile_rows(left_ref, right_ref, vectors_ref, high_ref, low_ref):
    width = 256
    total, waiting = 0.0, None
    for column in range(0, 2048 + width, width):
        made = None
        if column < 2048:
            across = slice(column, column + width)
            kernel = jnp.exp2(
                jnp.dot(left_ref[...], right_ref[:, across], preferred_element_type=F32)
            )
            high = kernel.astype(BF16)
            low = (kernel - high.astype(F32)).astype(BF16)
            high_ref[:, across] = high
            low_ref[:, across] = low
            made = across, high, low
        if waiting:
            across, *parts = waiting
            for part in parts:
                total = total + lax.dot_general(
                    vectors_ref[:, across], part, (((1,), (1,)), ((), ())),
                    preferred_element_type=F32,
                )
        waiting = made
    return sum_parts(total)


def sum_parts(total):
    return total[0:17] + total[32:49] + total[64:81]


def spread_kernel(points_hbm, sides_hbm, points_ref, sides_ref, copies_ref, done):
    copies = [
        pltpu.make_async_copy(points_hbm, points_ref, done.at[0]),
        pltpu.make_async_copy(sides_hbm, sides_ref, done.at[1]),
    ]
    for copy in copies:
        copy.start()
    for copy in copies:
        copy.wait()
    for k in range(16):
        copies_ref[k, 0:16, :] = points_ref[...]
        copies_ref[k, 16:33, :] = sides_ref[...]


def make_left(points_ref, left_ref):
    left_ref[...] = left_rows(points_ref[...]).T.astype(BF16)


def make_right(columns_ref, right_ref, vectors_ref):
    for group in range(4):
        block = jnp.concatenate([columns_ref[group * 4 + k] for k in range(4)], axis=1)
        at = slice(group * 512, group * 512 + 512)
        right_ref[:, at] = right_rows(block[:16]).astype(BF16)
        parts = [pad_rows(part, 32) for part in split3(block[16:])]
        vectors_ref[:, at] = jnp.concatenate(parts, axis=0).astype(BF16)


def near_own_kernel(
    points_ref, columns_ref, high_ref, low_ref, out_ref, left_ref, right_ref, vectors_ref
):
    make_left(points_ref, left_ref)
    make_right(columns_ref, right_ref, vectors_ref)
    out_ref[...] = tile_rows(left_ref, right_ref, vectors_ref, high_ref, low_ref)


def next_own_kernel(
    points_ref, right_ref, vectors_ref, high_ref, low_ref, out_ref, left_ref
):
    make_left(points_ref, left_ref)
    out_ref[...] = tile_rows(left_ref, right_ref, vectors_ref, high_ref, low_ref)


def next_other_kernel(
    left_ref, columns_ref, before_ref, high_ref, low_ref, out_ref, right_ref, vectors_ref
):
    make_right(columns_ref, right_ref, vectors_ref)
    out_ref[...] = before_ref[...] + tile_rows(
        left_ref, right_ref, vectors_ref, high_ref, low_ref
    )


def near_other_kernel(
    left_ref, right_ref, vectors_ref, before_ref, high_ref, low_ref, out_ref
):
    out_ref[...] = before_ref[...] + tile_rows(
        left_ref, right_ref, vectors_ref, high_ref, low_ref
    )


def stack_kernel(sum_ref, from_p_ref, out_ref):
    total = sum_ref[...] + from_p_ref[...]
    for k in range(4):
        out_ref[17 * k : 17 * k + 17, :] = total[:, 128 * k : 128 * k + 128]


def image_kernel(own_ref, one_ref, two_ref, three_ref, out_ref):
    for k in range(4):
        total = own_ref[17 * k : 17 * k + 17, :]
        for distance, ref in ((1, one_ref), (2, two_ref), (3, three_ref)):
            at = 17 * (k ^ distance)
            total = total + ref[at : at + 17, :]
        out_ref[:, 128 * k : 128 * k + 128] = total


def vector_parts(image_ref):
    return jnp.concatenate(
        [pad_rows(part, 32) for part in split3(image_ref[...])], axis=0
    ).astype(BF16)


def transposed_product(left, high_ref, low_ref):
    return sum_parts(
        jnp.dot(left, high_ref[...], preferred_element_type=F32)
        + jnp.dot(left, low_ref[...], preferred_element_type=F32)
    )


def near_transposed_kernel(
    image_ref, other_high_ref, other_low_ref, own_high_ref, own_low_ref, other_ref, own_ref
):
    left = vector_parts(image_ref)
    for high_ref, low_ref, out_ref in (
        (other_high_ref, other_low_ref, other_ref), (own_high_ref, own_low_ref, own_ref)
    ):
        total = transposed_product(left, high_ref, low_ref)
        for k in range(16):
            out_ref[k] = total[:, k * 128 : (k + 1) * 128]


def next_transposed_kernel(image_ref, high_ref, low_ref, before_ref, out_ref):
    total = transposed_product(vector_parts(image_ref), high_ref, low_ref)
    for k in range(16):
        out_ref[k] = before_ref[k] + total[:, k * 128 : (k + 1) * 128]


def dots_kernel(parts_ref, sides_ref, image_ref, out_first_ref, out_second_ref, dots_ref):
    sides = sides_ref[...]
    image = image_ref[:, :128]
    first = image - sides
    second = jnp.sum(parts_ref[...], axis=0) - image - first
    out_first_ref[...] = first
    out_second_ref[...] = second
    rows = jnp.concatenate(
        [pad_rows(t, 32) for t in (sides * sides, sides * first, first * first, first * second)],
        axis=0,
    )
    dots_ref[...] = jnp.sum(rows.T, axis=0, keepdims=True)


def last_kernel(dots_ref, sides_ref, first_ref, second_ref, solution_ref, residual_ref):
    dots = jnp.sum(dots_ref[...], axis=0)
    table = jnp.broadcast_to(dots, (128, 128)).T
    g0, g1, g2, g3 = (table[32 * k : 32 * k + 17] for k in range(4))
    diagonal = 1.0 + NOISE
    sides, first, second = sides_ref[...], first_ref[...], second_ref[...]
    step = g0 / (g1 + diagonal * g0)
    ratio = g1 / g0
    residual = step * (ratio * sides - first)
    norm = step * step * (g2 - ratio * g1)
    turn = norm / g0
    weight = step * ratio + turn
    direction = residual + turn * sides
    curve = (
        weight * weight * g1
        - 2.0 * weight * step * g2
        + step * step * g3
        + diagonal * (norm + turn * turn * g0)
    )
    step_next = norm / curve
    mapped = weight * first - step * second + diagonal * direction
    solution_ref[...] = step * sides + step_next * direction
    residual_ref[...] = residual - step_next * mapped


VMEM = pl.BlockSpec(memory_space=pltpu.VMEM)


def call(kernel, name, out_shape, scratch=(), flops=0, transcendentals=0):
    return pl.pallas_call(
        kernel,
        out_shape=out_shape,
        scratch_shapes=scratch,
        compiler_params=pltpu.CompilerParams(vmem_limit_bytes=28 * 1024 * 1024),
        cost_estimate=pl.CostEstimate(
            flops=flops, bytes_accessed=0, transcendentals=transcendentals
        ),
        name=name,
    )


def per_device(points, right_sides):
    permute = functools.partial(lax.ppermute, axis_name=AXES)
    exchange = functools.partial(
        lax.all_to_all, axis_name=AXES, split_axis=0, concat_axis=0, tiled=True
    )
    column_groups = groups_over("y", "x")
    swap_c, swap_p, swap_v, swap_uv = swap("c"), swap("p"), swap("v"), swap("u", "v")

    def shape(*dims, dtype=F32):
        return jax.ShapeDtypeStruct(dims, dtype)

    tiles = [pltpu.VMEM((512, 2048), BF16), pltpu.VMEM((512, 2048), BF16)]
    left_shape = shape(512, 128, dtype=BF16)
    right_shapes = [shape(128, 2048, dtype=BF16), shape(96, 2048, dtype=BF16)]
    make = functools.partial(
        call,
        flops=512 * 2048 * 128 * 6,
        transcendentals=512 * 2048,
    )

    by_v = permute(points, perm=swap_v)
    points, sides, copies = pl.pallas_call(
        spread_kernel,
        in_specs=[pl.BlockSpec(memory_space=pl.ANY)] * 2,
        out_shape=[
            pltpu.VMEM((16, 128), F32), pltpu.VMEM((17, 128), F32),
            pltpu.VMEM((16, 33, 128), F32),
        ],
        scratch_shapes=[pltpu.SemaphoreType.DMA((2,))],
        name="spread",
    )(points, right_sides)
    pair = jnp.concatenate([points, by_v], axis=1)
    near_points = jnp.concatenate([pair, permute(pair, perm=swap_uv)], axis=1)
    own = exchange(copies, axis_index_groups=column_groups)
    next_points = permute(near_points, perm=swap_p)
    own, near_points = lax.optimization_barrier((own, near_points))

    other = permute(own, perm=swap_c)
    *near_own, near_sum, near_left, right, vectors = make(
        near_own_kernel, "near_own",
        [*tiles, shape(17, 512), left_shape, *right_shapes],
    )(near_points, own)
    *next_own, next_sum, next_left = make(
        next_own_kernel, "next_own", [*tiles, shape(17, 512), left_shape]
    )(next_points, right, vectors)
    *next_other, next_sum, right, vectors = make(
        next_other_kernel, "next_other", [*tiles, shape(17, 512), *right_shapes]
    )(next_left, other, next_sum)
    from_p = permute(next_sum, perm=swap_p)
    *near_other, near_sum = make(
        near_other_kernel, "near_other", [*tiles, shape(17, 512)]
    )(near_left, right, vectors, near_sum)

    total = call(stack_kernel, "stack", shape(68, 128))(near_sum, from_p)
    image = call(image_kernel, "image", shape(17, 512))(
        total, *(permute(total, perm=p) for p in (swap_v, swap_uv, swap("u")))
    )

    by_owner = shape(16, 17, 128)
    next_image = permute(image, perm=swap_p)
    other_part, own_part = call(
        near_transposed_kernel, "near_transposed", [by_owner, by_owner],
        flops=1024 * 2048 * 512,
    )(image, *near_other, *near_own)
    product = functools.partial(
        call, next_transposed_kernel, out_shape=by_owner, flops=512 * 2048 * 512
    )
    other_part = product(name="other_transposed")(next_image, *next_other, other_part)
    from_c = permute(other_part, perm=swap_c)
    own_part = product(name="own_transposed")(next_image, *next_own, own_part)
    pieces = exchange(own_part + from_c, axis_index_groups=column_groups)

    vector = shape(17, 128)
    first, second, dots = call(dots_kernel, "dots", [vector, vector, shape(1, 128)])(
        pieces, sides, image
    )
    dots = dots + permute(dots, perm=swap_c)
    all_dots = exchange(
        jnp.broadcast_to(dots[None], (128, 1, 128)),
        axis_index_groups=groups_over("y", "u", "v", "p", "x"),
    )
    return call(last_kernel, "finish", [vector, vector])(
        all_dots, sides, first, second
    )


def solution(mesh):
    spec = P(None, ("col", "row"))
    return jax.shard_map(
        lambda p, r: tuple(per_device(p, r)),
        mesh=mesh,
        in_specs=(spec, spec),
        out_specs=(spec, spec),
        check_vma=False,
    )
```

```python
import functools
import math

import jax
import jax.numpy as jnp
import numpy as np
from jax import lax
from jax.experimental import pallas as pl
from jax.experimental.pallas import tpu as pltpu
from jax.sharding import PartitionSpec as P

AXES = ("row", "col")
NOISE = 0.1
SCALE = 0.125
COEF = SCALE * math.log2(math.e)
F32 = jnp.float32
BF16 = jnp.bfloat16

DIMS = (("y", 4), ("u", 2), ("v", 2), ("p", 2), ("x", 4), ("c", 2))
NAMES = [n for n, _ in DIMS]
IDS = np.arange(256).reshape([s for _, s in DIMS])


def swap(*names):
    target = np.flip(IDS, [NAMES.index(n) for n in names])
    return list(zip(IDS.reshape(-1).tolist(), target.reshape(-1).tolist()))


def groups_over(*names):
    rest = [n for n in NAMES if n not in names]
    order = [NAMES.index(n) for n in rest + list(names)]
    size = int(np.prod([dict(DIMS)[n] for n in names]))
    return IDS.transpose(order).reshape(-1, size).tolist()


def split3(value):
    first = value.astype(BF16).astype(F32)
    rest = value - first
    second = rest.astype(BF16).astype(F32)
    return first, second, (rest - second).astype(BF16).astype(F32)


def norm_rows(points, norm_first):
    norm = -COEF * jnp.sum(points * points, axis=0, keepdims=True)
    parts = split3(norm)
    index = lax.broadcasted_iota(jnp.int32, points.shape, 0)
    base = 0 if norm_first else 3
    ones = 3 - base
    rows = jnp.where((index >= ones) & (index < ones + 3), 1.0, 0.0)
    for k in range(3):
        rows = jnp.where(index == base + k, parts[k], rows)
    return rows


def left_rows(points):
    a, b, c = split3(points * (2.0 * COEF))
    return jnp.concatenate(
        [a, a, b, b, a, c, norm_rows(points, True), jnp.zeros_like(a)], axis=0
    )


def right_rows(points):
    a, b, c = split3(points)
    return jnp.concatenate(
        [a, b, a, b, c, a, norm_rows(points, False), jnp.zeros_like(a)], axis=0
    )


def pad_rows(value, rows):
    return jnp.concatenate(
        [value, jnp.zeros((rows - value.shape[0], value.shape[1]), value.dtype)], axis=0
    )


def tile_rows(left_ref, right_ref, vectors_ref, high_ref, low_ref):
    width = 256
    total, waiting = 0.0, None
    for column in range(0, 2048 + width, width):
        made = None
        if column < 2048:
            across = slice(column, column + width)
            kernel = jnp.exp2(
                jnp.dot(left_ref[...], right_ref[:, across], preferred_element_type=F32)
            )
            high = kernel.astype(BF16)
            low = (kernel - high.astype(F32)).astype(BF16)
            high_ref[:, across] = high
            low_ref[:, across] = low
            made = across, high, low
        if waiting:
            across, *parts = waiting
            for part in parts:
                total = total + lax.dot_general(
                    vectors_ref[:, across], part, (((1,), (1,)), ((), ())),
                    preferred_element_type=F32,
                )
        waiting = made
    return sum_parts(total)


def sum_parts(total):
    return total[0:17] + total[32:49] + total[64:81]


def spread_kernel(points_hbm, sides_hbm, points_ref, sides_ref, copies_ref, done):
    copies = [
        pltpu.make_async_copy(points_hbm, points_ref, done.at[0]),
        pltpu.make_async_copy(sides_hbm, sides_ref, done.at[1]),
    ]
    for copy in copies:
        copy.start()
    for copy in copies:
        copy.wait()
    for k in range(16):
        copies_ref[k, 0:16, :] = points_ref[...]
        copies_ref[k, 16:33, :] = sides_ref[...]


def make_left(points_ref, left_ref):
    left_ref[...] = left_rows(points_ref[...]).T.astype(BF16)


def make_right(columns_ref, right_ref, vectors_ref):
    for group in range(4):
        block = jnp.concatenate([columns_ref[group * 4 + k] for k in range(4)], axis=1)
        at = slice(group * 512, group * 512 + 512)
        right_ref[:, at] = right_rows(block[:16]).astype(BF16)
        parts = [pad_rows(part, 32) for part in split3(block[16:])]
        vectors_ref[:, at] = jnp.concatenate(parts, axis=0).astype(BF16)


def near_own_kernel(
    points_ref, columns_ref, high_ref, low_ref, out_ref, left_ref, right_ref, vectors_ref
):
    make_left(points_ref, left_ref)
    make_right(columns_ref, right_ref, vectors_ref)
    out_ref[...] = tile_rows(left_ref, right_ref, vectors_ref, high_ref, low_ref)


def next_own_kernel(
    points_ref, right_ref, vectors_ref, high_ref, low_ref, out_ref, left_ref
):
    make_left(points_ref, left_ref)
    out_ref[...] = tile_rows(left_ref, right_ref, vectors_ref, high_ref, low_ref)


def next_other_kernel(
    left_ref, columns_ref, before_ref, high_ref, low_ref, out_ref, right_ref, vectors_ref
):
    make_right(columns_ref, right_ref, vectors_ref)
    total = before_ref[...] + tile_rows(
        left_ref, right_ref, vectors_ref, high_ref, low_ref
    )
    for k in range(4):
        out_ref[17 * k : 17 * k + 17, :] = total[:, 128 * k : 128 * k + 128]


def near_other_kernel(
    left_ref, right_ref, vectors_ref, before_ref, high_ref, low_ref, out_ref
):
    out_ref[...] = before_ref[...] + tile_rows(
        left_ref, right_ref, vectors_ref, high_ref, low_ref
    )


def stack_kernel(sum_ref, from_p_ref, out_ref):
    for k in range(4):
        at = slice(17 * k, 17 * k + 17)
        out_ref[at, :] = sum_ref[:, 128 * k : 128 * k + 128] + from_p_ref[at, :]


def image_kernel(own_ref, one_ref, two_ref, three_ref, out_ref, packed_ref):
    for k in range(4):
        total = own_ref[17 * k : 17 * k + 17, :]
        for distance, ref in ((1, one_ref), (2, two_ref), (3, three_ref)):
            at = 17 * (k ^ distance)
            total = total + ref[at : at + 17, :]
        out_ref[:, 128 * k : 128 * k + 128] = total
        packed_ref[17 * k : 17 * k + 17, :] = total


def vector_parts(image):
    return jnp.concatenate(
        [pad_rows(part, 32) for part in split3(image)], axis=0
    ).astype(BF16)


def transposed_product(left, high_ref, low_ref):
    return sum_parts(
        jnp.dot(left, high_ref[...], preferred_element_type=F32)
        + jnp.dot(left, low_ref[...], preferred_element_type=F32)
    )


def near_transposed_kernel(
    image_ref, other_high_ref, other_low_ref, own_high_ref, own_low_ref, other_ref, own_ref
):
    left = vector_parts(image_ref[...])
    for high_ref, low_ref, out_ref in (
        (other_high_ref, other_low_ref, other_ref), (own_high_ref, own_low_ref, own_ref)
    ):
        total = transposed_product(left, high_ref, low_ref)
        for k in range(16):
            out_ref[k] = total[:, k * 128 : (k + 1) * 128]


def next_transposed_kernel(image_ref, high_ref, low_ref, before_ref, out_ref):
    total = transposed_product(vector_parts(
        jnp.concatenate([image_ref[17 * k : 17 * k + 17, :] for k in range(4)], axis=1)
    ), high_ref, low_ref)
    for k in range(16):
        out_ref[k] = before_ref[k] + total[:, k * 128 : (k + 1) * 128]


def dots_kernel(parts_ref, sides_ref, image_ref, out_first_ref, out_second_ref, dots_ref):
    sides = sides_ref[...]
    image = image_ref[:, :128]
    first = image - sides
    second = jnp.sum(parts_ref[...], axis=0) - image - first
    out_first_ref[...] = first
    out_second_ref[...] = second
    rows = jnp.concatenate(
        [pad_rows(t, 32) for t in (sides * sides, sides * first, first * first, first * second)],
        axis=0,
    )
    dots_ref[...] = jnp.sum(rows.T, axis=0, keepdims=True)


def last_kernel(dots_ref, sides_ref, first_ref, second_ref, solution_ref, residual_ref):
    dots = jnp.sum(dots_ref[...], axis=0)
    table = jnp.broadcast_to(dots, (128, 128)).T
    g0, g1, g2, g3 = (table[32 * k : 32 * k + 17] for k in range(4))
    diagonal = 1.0 + NOISE
    sides, first, second = sides_ref[...], first_ref[...], second_ref[...]
    step = g0 / (g1 + diagonal * g0)
    ratio = g1 / g0
    residual = step * (ratio * sides - first)
    norm = step * step * (g2 - ratio * g1)
    turn = norm / g0
    weight = step * ratio + turn
    direction = residual + turn * sides
    curve = (
        weight * weight * g1
        - 2.0 * weight * step * g2
        + step * step * g3
        + diagonal * (norm + turn * turn * g0)
    )
    step_next = norm / curve
    mapped = weight * first - step * second + diagonal * direction
    solution_ref[...] = step * sides + step_next * direction
    residual_ref[...] = residual - step_next * mapped


VMEM = pl.BlockSpec(memory_space=pltpu.VMEM)


def call(kernel, name, out_shape, scratch=(), flops=0, transcendentals=0):
    return pl.pallas_call(
        kernel,
        out_shape=out_shape,
        scratch_shapes=scratch,
        compiler_params=pltpu.CompilerParams(vmem_limit_bytes=28 * 1024 * 1024),
        cost_estimate=pl.CostEstimate(
            flops=flops, bytes_accessed=0, transcendentals=transcendentals
        ),
        name=name,
    )


def per_device(points, right_sides):
    permute = functools.partial(lax.ppermute, axis_name=AXES)
    exchange = functools.partial(
        lax.all_to_all, axis_name=AXES, split_axis=0, concat_axis=0, tiled=True
    )
    column_groups = groups_over("y", "x")
    swap_c, swap_p, swap_v, swap_uv = swap("c"), swap("p"), swap("v"), swap("u", "v")

    def shape(*dims, dtype=F32):
        return jax.ShapeDtypeStruct(dims, dtype)

    tiles = [pltpu.VMEM((512, 2048), BF16), pltpu.VMEM((512, 2048), BF16)]
    left_shape = shape(512, 128, dtype=BF16)
    right_shapes = [shape(128, 2048, dtype=BF16), shape(96, 2048, dtype=BF16)]
    make = functools.partial(
        call,
        flops=512 * 2048 * 128 * 6,
        transcendentals=512 * 2048,
    )

    by_v = permute(points, perm=swap_v)
    points, sides, copies = pl.pallas_call(
        spread_kernel,
        in_specs=[pl.BlockSpec(memory_space=pl.ANY)] * 2,
        out_shape=[
            pltpu.VMEM((16, 128), F32), pltpu.VMEM((17, 128), F32),
            pltpu.VMEM((16, 33, 128), F32),
        ],
        scratch_shapes=[pltpu.SemaphoreType.DMA((2,))],
        name="spread",
    )(points, right_sides)
    pair = jnp.concatenate([points, by_v], axis=1)
    near_points = jnp.concatenate([pair, permute(pair, perm=swap_uv)], axis=1)
    own = exchange(copies, axis_index_groups=column_groups)
    next_points = permute(near_points, perm=swap_p)
    own, near_points = lax.optimization_barrier((own, near_points))

    other = permute(own, perm=swap_c)
    *near_own, near_sum, near_left, right, vectors = make(
        near_own_kernel, "near_own",
        [*tiles, shape(17, 512), left_shape, *right_shapes],
    )(near_points, own)
    *next_own, next_sum, next_left = make(
        next_own_kernel, "next_own", [*tiles, shape(17, 512), left_shape]
    )(next_points, right, vectors)
    *next_other, next_sum, right, vectors = make(
        next_other_kernel, "next_other", [*tiles, shape(68, 128), *right_shapes]
    )(next_left, other, next_sum)
    from_p = permute(next_sum, perm=swap_p)
    *near_other, near_sum = make(
        near_other_kernel, "near_other", [*tiles, shape(17, 512)]
    )(near_left, right, vectors, near_sum)

    total = call(stack_kernel, "stack", shape(68, 128))(near_sum, from_p)
    image, packed = call(image_kernel, "image", [shape(17, 512), shape(68, 128)])(
        total, *(permute(total, perm=p) for p in (swap_v, swap_uv, swap("u")))
    )

    by_owner = shape(16, 17, 128)
    next_image = permute(packed, perm=swap_p)
    other_part, own_part = call(
        near_transposed_kernel, "near_transposed", [by_owner, by_owner],
        flops=1024 * 2048 * 512,
    )(image, *near_other, *near_own)
    product = functools.partial(
        call, next_transposed_kernel, out_shape=by_owner, flops=512 * 2048 * 512
    )
    other_part = product(name="other_transposed")(next_image, *next_other, other_part)
    from_c = permute(other_part, perm=swap_c)
    own_part = product(name="own_transposed")(next_image, *next_own, own_part)
    pieces = exchange(own_part + from_c, axis_index_groups=column_groups)

    vector = shape(17, 128)
    first, second, dots = call(dots_kernel, "dots", [vector, vector, shape(1, 128)])(
        pieces, sides, image
    )
    dots = dots + permute(dots, perm=swap_c)
    all_dots = exchange(
        jnp.broadcast_to(dots[None], (128, 1, 128)),
        axis_index_groups=groups_over("y", "u", "v", "p", "x"),
    )
    return call(last_kernel, "finish", [vector, vector])(
        all_dots, sides, first, second
    )


def solution(mesh):
    spec = P(None, ("col", "row"))
    return jax.shard_map(
        lambda p, r: tuple(per_device(p, r)),
        mesh=mesh,
        in_specs=(spec, spec),
        out_specs=(spec, spec),
        check_vma=False,
    )
```

```python
import functools
import math

import jax
import jax.numpy as jnp
import numpy as np
from jax import lax
from jax.experimental import pallas as pl
from jax.experimental.pallas import tpu as pltpu
from jax.sharding import PartitionSpec as P

AXES = ("row", "col")
NOISE = 0.1
SCALE = 0.125
COEF = SCALE * math.log2(math.e)
F32 = jnp.float32
BF16 = jnp.bfloat16

DIMS = (("y", 4), ("u", 2), ("v", 2), ("p", 2), ("x", 4), ("c", 2))
NAMES = [n for n, _ in DIMS]
IDS = np.arange(256).reshape([s for _, s in DIMS])


def swap(*names):
    target = np.flip(IDS, [NAMES.index(n) for n in names])
    return list(zip(IDS.reshape(-1).tolist(), target.reshape(-1).tolist()))


def by_core(even, odd):
    return [(a if d % 2 == 0 else b) for d, (a, b) in enumerate(zip(even, odd))]


def groups_over(*names):
    rest = [n for n in NAMES if n not in names]
    order = [NAMES.index(n) for n in rest + list(names)]
    size = int(np.prod([dict(DIMS)[n] for n in names]))
    return IDS.transpose(order).reshape(-1, size).tolist()


def split3(value):
    first = value.astype(BF16).astype(F32)
    rest = value - first
    second = rest.astype(BF16).astype(F32)
    return first, second, (rest - second).astype(BF16).astype(F32)


def norm_rows(points, norm_first):
    norm = -COEF * jnp.sum(points * points, axis=0, keepdims=True)
    parts = split3(norm)
    index = lax.broadcasted_iota(jnp.int32, points.shape, 0)
    base = 0 if norm_first else 3
    ones = 3 - base
    rows = jnp.where((index >= ones) & (index < ones + 3), 1.0, 0.0)
    for k in range(3):
        rows = jnp.where(index == base + k, parts[k], rows)
    return rows


def left_rows(points):
    a, b, c = split3(points * (2.0 * COEF))
    return jnp.concatenate(
        [a, a, b, b, a, c, norm_rows(points, True), jnp.zeros_like(a)], axis=0
    )


def right_rows(points):
    a, b, c = split3(points)
    return jnp.concatenate(
        [a, b, a, b, c, a, norm_rows(points, False), jnp.zeros_like(a)], axis=0
    )


def pad_rows(value, rows):
    return jnp.concatenate(
        [value, jnp.zeros((rows - value.shape[0], value.shape[1]), value.dtype)], axis=0
    )


def tile_rows(left_ref, right_ref, vectors_ref, high_ref, low_ref):
    width = 256
    total, waiting = 0.0, None
    for column in range(0, 2048 + width, width):
        made = None
        if column < 2048:
            across = slice(column, column + width)
            kernel = jnp.exp2(
                jnp.dot(left_ref[...], right_ref[:, across], preferred_element_type=F32)
            )
            high = kernel.astype(BF16)
            low = (kernel - high.astype(F32)).astype(BF16)
            high_ref[:, across] = high
            low_ref[:, across] = low
            made = across, high, low
        if waiting:
            across, *parts = waiting
            for part in parts:
                total = total + lax.dot_general(
                    vectors_ref[:, across], part, (((1,), (1,)), ((), ())),
                    preferred_element_type=F32,
                )
        waiting = made
    return sum_parts(total)


def sum_parts(total):
    return total[0:17] + total[32:49] + total[64:81]


def spread_kernel(points_hbm, sides_hbm, points_ref, sides_ref, copies_ref, done):
    copies = [
        pltpu.make_async_copy(points_hbm, points_ref, done.at[0]),
        pltpu.make_async_copy(sides_hbm, sides_ref, done.at[1]),
    ]
    for copy in copies:
        copy.start()
    for copy in copies:
        copy.wait()
    for k in range(16):
        copies_ref[k, 0:16, :] = points_ref[...]
        copies_ref[k, 16:33, :] = sides_ref[...]


def make_left(points_ref, left_ref):
    left_ref[...] = left_rows(points_ref[...]).T.astype(BF16)


def make_right(columns_ref, right_ref, vectors_ref):
    for group in range(4):
        block = jnp.concatenate([columns_ref[group * 4 + k] for k in range(4)], axis=1)
        at = slice(group * 512, group * 512 + 512)
        right_ref[:, at] = right_rows(block[:16]).astype(BF16)
        parts = [pad_rows(part, 32) for part in split3(block[16:])]
        vectors_ref[:, at] = jnp.concatenate(parts, axis=0).astype(BF16)


def near_own_kernel(
    points_ref, columns_ref, high_ref, low_ref, out_ref, left_ref, right_ref, vectors_ref
):
    make_left(points_ref, left_ref)
    make_right(columns_ref, right_ref, vectors_ref)
    out_ref[...] = tile_rows(left_ref, right_ref, vectors_ref, high_ref, low_ref)


def next_own_kernel(
    points_ref, right_ref, vectors_ref, high_ref, low_ref, out_ref, left_ref
):
    make_left(points_ref, left_ref)
    out_ref[...] = tile_rows(left_ref, right_ref, vectors_ref, high_ref, low_ref)


def next_other_kernel(
    left_ref, columns_ref, before_ref, high_ref, low_ref, out_ref, right_ref, vectors_ref
):
    make_right(columns_ref, right_ref, vectors_ref)
    total = before_ref[...] + tile_rows(
        left_ref, right_ref, vectors_ref, high_ref, low_ref
    )
    for k in range(4):
        out_ref[17 * k : 17 * k + 17, :] = total[:, 128 * k : 128 * k + 128]


def near_other_kernel(
    left_ref, right_ref, vectors_ref, before_ref, high_ref, low_ref, out_ref
):
    out_ref[...] = before_ref[...] + tile_rows(
        left_ref, right_ref, vectors_ref, high_ref, low_ref
    )


def stack_kernel(sum_ref, from_p_ref, out_ref):
    for k in range(4):
        at = slice(17 * k, 17 * k + 17)
        out_ref[at, :] = sum_ref[:, 128 * k : 128 * k + 128] + from_p_ref[at, :]


def image_kernel(own_ref, one_ref, two_ref, three_ref, out_ref, packed_ref):
    for k in range(4):
        total = own_ref[17 * k : 17 * k + 17, :]
        for distance, ref in ((1, one_ref), (2, two_ref), (3, three_ref)):
            at = 17 * (k ^ distance)
            total = total + ref[at : at + 17, :]
        out_ref[:, 128 * k : 128 * k + 128] = total
        packed_ref[17 * k : 17 * k + 17, :] = total


def vector_parts(image):
    return jnp.concatenate(
        [pad_rows(part, 32) for part in split3(image)], axis=0
    ).astype(BF16)


def transposed_product(left, high_ref, low_ref):
    return sum_parts(
        jnp.dot(left, high_ref[...], preferred_element_type=F32)
        + jnp.dot(left, low_ref[...], preferred_element_type=F32)
    )


def near_transposed_kernel(
    image_ref, other_high_ref, other_low_ref, own_high_ref, own_low_ref, other_ref, own_ref
):
    left = vector_parts(image_ref[...])
    for high_ref, low_ref, out_ref in (
        (other_high_ref, other_low_ref, other_ref), (own_high_ref, own_low_ref, own_ref)
    ):
        total = transposed_product(left, high_ref, low_ref)
        for k in range(16):
            out_ref[k] = total[:, k * 128 : (k + 1) * 128]


def next_transposed_kernel(image_ref, high_ref, low_ref, before_ref, out_ref):
    total = transposed_product(vector_parts(
        jnp.concatenate([image_ref[17 * k : 17 * k + 17, :] for k in range(4)], axis=1)
    ), high_ref, low_ref)
    for k in range(16):
        out_ref[k] = before_ref[k] + total[:, k * 128 : (k + 1) * 128]


def dots_kernel(parts_ref, sides_ref, image_ref, out_first_ref, out_second_ref, dots_ref):
    sides = sides_ref[...]
    image = image_ref[:, :128]
    first = image - sides
    second = jnp.sum(parts_ref[...], axis=0) - image - first
    out_first_ref[...] = first
    out_second_ref[...] = second
    rows = jnp.concatenate(
        [pad_rows(t, 32) for t in (sides * sides, sides * first, first * first, first * second)],
        axis=0,
    )
    dots_ref[...] = jnp.sum(rows.T, axis=0, keepdims=True)


def last_kernel(dots_ref, sides_ref, first_ref, second_ref, solution_ref, residual_ref):
    dots = jnp.sum(dots_ref[...], axis=0)
    table = jnp.broadcast_to(dots, (128, 128)).T
    g0, g1, g2, g3 = (table[32 * k : 32 * k + 17] for k in range(4))
    diagonal = 1.0 + NOISE
    sides, first, second = sides_ref[...], first_ref[...], second_ref[...]
    step = g0 / (g1 + diagonal * g0)
    ratio = g1 / g0
    residual = step * (ratio * sides - first)
    norm = step * step * (g2 - ratio * g1)
    turn = norm / g0
    weight = step * ratio + turn
    direction = residual + turn * sides
    curve = (
        weight * weight * g1
        - 2.0 * weight * step * g2
        + step * step * g3
        + diagonal * (norm + turn * turn * g0)
    )
    step_next = norm / curve
    mapped = weight * first - step * second + diagonal * direction
    solution_ref[...] = step * sides + step_next * direction
    residual_ref[...] = residual - step_next * mapped


VMEM = pl.BlockSpec(memory_space=pltpu.VMEM)


def call(kernel, name, out_shape, scratch=(), flops=0, transcendentals=0):
    return pl.pallas_call(
        kernel,
        out_shape=out_shape,
        scratch_shapes=scratch,
        compiler_params=pltpu.CompilerParams(vmem_limit_bytes=28 * 1024 * 1024),
        cost_estimate=pl.CostEstimate(
            flops=flops, bytes_accessed=0, transcendentals=transcendentals
        ),
        name=name,
    )


def per_device(points, right_sides):
    permute = functools.partial(lax.ppermute, axis_name=AXES)
    exchange = functools.partial(
        lax.all_to_all, axis_name=AXES, split_axis=0, concat_axis=0, tiled=True
    )
    column_groups = groups_over("y", "x")
    swap_c, swap_p, swap_v, swap_uv = swap("c"), swap("p"), swap("v"), swap("u", "v")
    swap_v, swap_uv = by_core(swap_v, swap_uv), by_core(swap_uv, swap_v)

    def shape(*dims, dtype=F32):
        return jax.ShapeDtypeStruct(dims, dtype)

    tiles = [pltpu.VMEM((512, 2048), BF16), pltpu.VMEM((512, 2048), BF16)]
    left_shape = shape(512, 128, dtype=BF16)
    right_shapes = [shape(128, 2048, dtype=BF16), shape(96, 2048, dtype=BF16)]
    make = functools.partial(
        call,
        flops=512 * 2048 * 128 * 6,
        transcendentals=512 * 2048,
    )

    by_v = permute(points, perm=swap_v)
    points, sides, copies = pl.pallas_call(
        spread_kernel,
        in_specs=[pl.BlockSpec(memory_space=pl.ANY)] * 2,
        out_shape=[
            pltpu.VMEM((16, 128), F32), pltpu.VMEM((17, 128), F32),
            pltpu.VMEM((16, 33, 128), F32),
        ],
        scratch_shapes=[pltpu.SemaphoreType.DMA((2,))],
        name="spread",
    )(points, right_sides)
    pair = jnp.concatenate([points, by_v], axis=1)
    near_points = jnp.concatenate([pair, permute(pair, perm=swap_uv)], axis=1)
    own = exchange(copies, axis_index_groups=column_groups)
    next_points = permute(near_points, perm=swap_p)
    own, near_points = lax.optimization_barrier((own, near_points))

    other = permute(own, perm=swap_c)
    *near_own, near_sum, near_left, right, vectors = make(
        near_own_kernel, "near_own",
        [*tiles, shape(17, 512), left_shape, *right_shapes],
    )(near_points, own)
    *next_own, next_sum, next_left = make(
        next_own_kernel, "next_own", [*tiles, shape(17, 512), left_shape]
    )(next_points, right, vectors)
    *next_other, next_sum, right, vectors = make(
        next_other_kernel, "next_other", [*tiles, shape(68, 128), *right_shapes]
    )(next_left, other, next_sum)
    from_p = permute(next_sum, perm=swap_p)
    *near_other, near_sum = make(
        near_other_kernel, "near_other", [*tiles, shape(17, 512)]
    )(near_left, right, vectors, near_sum)

    total = call(stack_kernel, "stack", shape(68, 128))(near_sum, from_p)
    image, packed = call(image_kernel, "image", [shape(17, 512), shape(68, 128)])(
        total, *(permute(total, perm=p) for p in (swap_v, swap_uv, swap("u")))
    )

    by_owner = shape(16, 17, 128)
    next_image = permute(packed, perm=swap_p)
    other_part, own_part = call(
        near_transposed_kernel, "near_transposed", [by_owner, by_owner],
        flops=1024 * 2048 * 512,
    )(image, *near_other, *near_own)
    product = functools.partial(
        call, next_transposed_kernel, out_shape=by_owner, flops=512 * 2048 * 512
    )
    other_part = product(name="other_transposed")(next_image, *next_other, other_part)
    from_c = permute(other_part, perm=swap_c)
    own_part = product(name="own_transposed")(next_image, *next_own, own_part)
    pieces = exchange(own_part + from_c, axis_index_groups=column_groups)

    vector = shape(17, 128)
    first, second, dots = call(dots_kernel, "dots", [vector, vector, shape(1, 128)])(
        pieces, sides, image
    )
    dots = dots + permute(dots, perm=swap_c)
    all_dots = exchange(
        jnp.broadcast_to(dots[None], (128, 1, 128)),
        axis_index_groups=groups_over("y", "u", "v", "p", "x"),
    )
    return call(last_kernel, "finish", [vector, vector])(
        all_dots, sides, first, second
    )


def solution(mesh):
    spec = P(None, ("col", "row"))
    return jax.shard_map(
        lambda p, r: tuple(per_device(p, r)),
        mesh=mesh,
        in_specs=(spec, spec),
        out_specs=(spec, spec),
        check_vma=False,
    )
```
